128 devices in a mesh: gx: 16 (over z, x), gy: 8 (over y, core).
Axes of the slice: x: 4, y: 4, z: 4, core: 2. Of those that a mesh axis runs over, the one named last changes fastest.
Arguments:
- fields: float32 [5, 768, 512, 128], P(None, 'gx', 'gy'), may hold values from -6 to 9
- emission: float32 [16, 128, 4, 128], P('gx', 'gy'), may hold values from 0.2 to 5
- albedo: float32 [16, 128, 128], P('gx', 'gy'), may hold values from 0.1 to 0.7
- tile_faces: int32 [16, 128], P('gx', 'gy'), may hold values from 32 to 128
- face_cell: int32 [16, 128, 128], P('gx', 'gy'), may hold values from 0 to 393215, as said below
- src_tile: int32 [16, 512], P('gx', 'gy'), may hold values from 0 to 15
- dst_tile: int32 [16, 512], P('gx', 'gy'), may hold values from 0 to 127, as said below
- view_factor: float32 [16, 512, 128, 128], P('gx', 'gy'), may hold values from 0 to 0.06
- pair_count: int32 [16, 8], P('gx', 'gy'), may hold values from 16 to 64
- plane_index: int32 [16], P('gx'), may hold values from 0 to 47
Outputs:
- fields_out: float32 [5, 768, 512, 128], P(None, 'gx', 'gy')
- radiosity: float32 [16, 128, 4, 128], P('gx', 'gy')
The draws below stay inside these ranges and needn't reach their ends.
Inputs may be any that keep to these rules, and one draw needn't show every extreme that they name: `dst_tile`: of one device's live pairs at most 8 target tiles of one device of the gy axis, and in every draw some device has all 64 pairs live and 8 of them to each device. `face_cell`: faces heat cells in the lowest quarter of the levels.
All inputs are finite; a program needn't handle non-finite values.
Results may differ from the reference program's by a relative error of at most 0.00018.
Values sent between devices are 32-bit elements; how exact they have to be, the bound alone decides.
No kernel may reach another device: no remote copies, remote signals or barrier semaphores. Data moves between devices by JAX's collectives and lax.ppermute only.
A program may use at most 128 MiB of HBM per device.

```python
import math
import jax
import jax.numpy as jnp
from jax import lax

CX = 48
CY = 64
NZ = 128
STEPS = 4
REFL = 2
BANDS = 4
FACES = 128
TILES_DEV = 16
CAP = 8
PAIRS_DEV = 64
TILES = 128
PAIRS = 512
NX = 768
NY = 512
N_GX = 16
N_GY = 8


def draw_fields(key, part):
    key = jax.random.fold_in(key, 17)
    shape = (5, NX, NY, NZ)
    rough = jax.random.truncated_normal(key, -3.0, 3.0, shape, jnp.float32)
    means = jnp.array([0.0, 0.0, 5.0, 4.0, 0.0], jnp.float32)
    spread = jnp.array([1.3, 1.3, 1.0, 1.0, 1.0], jnp.float32)
    return (means[:, None, None, None] + spread[:, None, None, None] * rough).astype(jnp.float32)


def draw_view_factor(key, part):
    key = jax.random.fold_in(key, 19)
    first, second, third = jax.random.split(key, 3)
    slabs = NX // CX
    shape = (slabs, PAIRS, FACES, FACES)
    top = 10.0
    base = jax.random.uniform(first, shape, jnp.float32, 0.25, 1.0)
    rows = jnp.exp(jax.random.uniform(second, (slabs, PAIRS, FACES, 1), jnp.float32, 0.0, math.log(top)))
    cols = jnp.exp(jax.random.uniform(third, (slabs, PAIRS, 1, FACES), jnp.float32, 0.0, math.log(top)))
    return (0.03 / FACES * base * rows * cols).astype(jnp.float32)


def draw_face_cell(key, part):
    key = jax.random.fold_in(key, 13)
    first, second, third = jax.random.split(key, 3)
    shape = (N_GX, TILES, FACES)
    cell_a = jax.random.randint(first, shape, 0, CX)
    cell_c = jax.random.randint(second, shape, 0, CY)
    cell_k = jax.random.randint(third, shape, 0, NZ // 4)
    return ((cell_a * CY + cell_c) * NZ + cell_k).astype(jnp.int32)


def draw_dst_tile(key, part):
    key = jax.random.fold_in(key, 7)
    keys = jax.random.split(key, N_GX * N_GY)

    def one_device(sub):
        first, second = jax.random.split(sub)
        order = jax.random.permutation(first, PAIRS_DEV)
        device = order // CAP
        tile = jax.random.randint(second, (PAIRS_DEV,), 0, TILES_DEV)
        return device * TILES_DEV + tile
    return jax.vmap(one_device)(keys).reshape(N_GX, N_GY * PAIRS_DEV).astype(jnp.int32)


def draw_pair_count(key, part):
    key = jax.random.fold_in(key, 11)
    first, second = jax.random.split(key)
    counts = jax.random.randint(first, (N_GX * N_GY,), PAIRS_DEV // 4, PAIRS_DEV + 1)
    where_full = jax.random.randint(second, (), 0, N_GX * N_GY)
    counts = counts.at[where_full].set(PAIRS_DEV)
    return counts.reshape(N_GX, N_GY).astype(jnp.int32)


def touch_ends(values, own_key, least, largest):
    extent = values.shape
    index_at = [jax.random.randint(jax.random.fold_in(own_key, axis), (), 0, extent[axis]) for axis in range(len(extent))]
    values = values.at[tuple(index_at)].set(least)
    longest = extent.index(max(extent))
    index_at[longest] = (index_at[longest] + 1) % extent[longest]
    return values.at[tuple(index_at)].set(largest)


def levels(key, dims, pieces, least, high):
    factor_of, own = 1.0, jax.random.fold_in(key, 6)
    for axis_at, shards_of in pieces:
        heights = jnp.exp(jax.random.uniform(jax.random.fold_in(own, axis_at), (shards_of,), jnp.float32, least / len(pieces), high / len(pieces)))
        factor_of = factor_of * jnp.repeat(heights, dims[axis_at] // shards_of).reshape([-1 if axis == axis_at else 1 for axis in range(len(dims))])
    return factor_of


def setup_inputs(seed: int = 0) -> dict:
    arg_keys = jax.random.split(jax.random.key(seed), 11)
    return {
        "fields": draw_fields(jax.random.fold_in(arg_keys[10], 71), 0),
        "emission": jnp.clip(jnp.exp(math.log(5.0) - 3.218876 * jax.random.uniform(arg_keys[1], (NX // CX, TILES, BANDS, FACES), jnp.float32) ** levels(arg_keys[1], (NX // CX, TILES, BANDS, FACES), ((0, 16), (1, 8)), -0.2, 0.2)), 0.2, 5.0),
        "albedo": jnp.clip(0.1 + 0.59999999 * jax.random.uniform(arg_keys[2], (NX // CX, TILES, FACES), jnp.float32) ** levels(arg_keys[2], (NX // CX, TILES, FACES), ((0, 16), (1, 8)), -0.2, 0.2), 0.1, 0.7),
        "tile_faces": touch_ends(jax.random.randint(arg_keys[3], (NX // CX, TILES), FACES // 4, FACES + 1), jax.random.fold_in(arg_keys[3], 1), FACES // 4, FACES).astype(jnp.int32),
        "face_cell": draw_face_cell(jax.random.fold_in(arg_keys[10], 71), 0),
        "src_tile": touch_ends(jax.random.randint(arg_keys[5], (NX // CX, PAIRS), 0, TILES_DEV), jax.random.fold_in(arg_keys[5], 1), 0, TILES_DEV - 1).astype(jnp.int32),
        "dst_tile": draw_dst_tile(jax.random.fold_in(arg_keys[10], 71), 0),
        "view_factor": draw_view_factor(jax.random.fold_in(arg_keys[10], 71), 0),
        "pair_count": draw_pair_count(jax.random.fold_in(arg_keys[10], 71), 0),
        "plane_index": touch_ends(jax.random.randint(arg_keys[9], (NX // CX,), 0, CX), jax.random.fold_in(arg_keys[9], 1), 0, CX - 1).astype(jnp.int32),
    }


HIGH = lax.Precision.HIGHEST


def advance(padded, heating, recycled):
    center = padded[:, 1:-1, 1:-1, 1:-1]
    xplus = padded[:, 2:, 1:-1, 1:-1]
    xminus = padded[:, :-2, 1:-1, 1:-1]
    yplus = padded[:, 1:-1, 2:, 1:-1]
    yminus = padded[:, 1:-1, :-2, 1:-1]
    zplus = padded[:, 1:-1, 1:-1, 2:]
    zminus = padded[:, 1:-1, 1:-1, :-2]
    advect = 0.5 * (center[2] * (xplus - xminus) + center[3] * (yplus - yminus) + center[4] * (zplus - zminus))
    laplace = xplus + xminus + yplus + yminus + zplus + zminus - 6.0 * center
    fresh = center + 0.1 * (0.2 * laplace - advect) + 0.05 * (recycled - center)
    return fresh.at[0].add(0.1 * heating)


def reference(fields, emission, albedo, tile_faces, face_cell, src_tile, dst_tile, view_factor, pair_count, plane_index):
    faces_idx = jnp.arange(FACES, dtype=jnp.int32)
    live = (faces_idx[None, None, :] < tile_faces[:, :, None]).astype(jnp.float32)
    pair_idx = jnp.arange(PAIRS, dtype=jnp.int32)
    owner = pair_idx // PAIRS_DEV
    source = owner[None, :] * TILES_DEV + src_tile
    valid = ((pair_idx % PAIRS_DEV)[None, :] < pair_count[:, owner]).astype(jnp.float32)
    tile_idx = jnp.arange(TILES, dtype=jnp.int32)
    target = (dst_tile[:, None, :] == tile_idx[None, :, None]).astype(jnp.float32) * valid[:, None, :]
    radiosity = live[:, :, None, :] * emission
    incoming = jnp.zeros_like(radiosity)
    for round_idx in range(REFL):
        picked = jnp.take_along_axis(radiosity, source[:, :, None, None], axis=1)
        contrib = jnp.einsum("gpij,gpbj->gpbi", view_factor, picked, precision=HIGH)
        incoming = jnp.einsum("gtp,gpbi->gtbi", target, contrib, precision=HIGH)
        radiosity = live[:, :, None, :] * (emission + albedo[:, :, None, :] * incoming)
    absorbed = live * (1.0 - albedo) * jnp.sum(incoming, axis=2)
    slabs = NX // CX
    slab = jnp.arange(slabs, dtype=jnp.int32)[:, None, None]
    owner_y = (tile_idx // TILES_DEV)[None, :, None]
    cell_a = face_cell // (CY * NZ)
    cell_c = (face_cell // NZ) % CY
    cell_k = face_cell % NZ
    flat = ((slab * CX + cell_a) * NY + owner_y * CY + cell_c) * NZ + cell_k
    heating = jnp.zeros((NX * NY * NZ,), jnp.float32).at[flat.reshape(-1)].add(absorbed.reshape(-1))
    heating = heating.reshape(NX, NY, NZ)
    source_slab = (jnp.arange(slabs, dtype=jnp.int32) + slabs // 2) % slabs
    columns = (source_slab * CX + plane_index[source_slab]).astype(jnp.int32)
    planes = jnp.take(fields, columns, axis=1)
    recycled = jnp.repeat(planes, CX, axis=1)
    current = fields
    for step_idx in range(STEPS):
        padded = jnp.pad(current, ((0, 0), (1, 1), (1, 1), (1, 1)))
        current = advance(padded, heating, recycled)
    return current, radiosity
```

```python
import jax
import jax.numpy as jnp
from jax import lax
from jax.experimental import pallas as pl
from jax.experimental.pallas import tpu as pltpu
from jax.sharding import PartitionSpec as P

STEPS = 4
REFL = 2
FACES = 128
TILES_DEV = 16
CAP = 8
HALO = STEPS
CHUNK = 8

HIGH = lax.Precision.HIGHEST


def shifted(value, axis, steps, wrap=False):
    count = lax.axis_size(axis)
    pairs = [(i, (i + steps) % count) for i in range(count) if wrap or 0 <= i + steps < count]
    return lax.ppermute(value, axis, pairs)


def stencil_kernel(
    fields, yside, xlow, xhigh, planes, heat, out, a, b, rec, src, in_sems, out_sems, *, width, rows
):
    fields_n = fields.shape[0]
    tiles = rows // 8 + 1
    chunks = width // CHUNK
    total = width + 2 * HALO
    gx = lax.axis_index("gx")
    gy = lax.axis_index("gy")
    last_gx = lax.axis_size("gx") - 1
    last_gy = lax.axis_size("gy") - 1

    def own_copy(k):
        return pltpu.make_async_copy(
            fields.at[:, pl.ds(k * CHUNK, CHUNK)],
            a.at[:, pl.ds(HALO + k * CHUNK, CHUNK), pl.ds(0, rows)],
            in_sems.at[0, k],
        )

    def side_copy(k):
        return pltpu.make_async_copy(
            yside.at[:, pl.ds(k * CHUNK, CHUNK)],
            a.at[:, pl.ds(HALO + k * CHUNK, CHUNK), pl.ds(rows, 8)],
            in_sems.at[1, k],
        )

    def out_copy(k):
        return pltpu.make_async_copy(
            a.at[:, pl.ds(HALO + k * CHUNK, CHUNK), pl.ds(0, rows)],
            out.at[:, pl.ds(k * CHUNK, CHUNK)],
            out_sems.at[k],
        )

    low_copy = pltpu.make_async_copy(xlow, a.at[:, pl.ds(0, HALO)], in_sems.at[2, 0])
    high_copy = pltpu.make_async_copy(xhigh, a.at[:, pl.ds(HALO + width, HALO)], in_sems.at[2, 1])
    plane_copy = pltpu.make_async_copy(planes, rec, in_sems.at[2, 2])
    heat_copy = pltpu.make_async_copy(heat, src, in_sems.at[2, 3])
    plane_copy.start()
    low_copy.start()
    heat_copy.start()
    for k in range(chunks):
        own_copy(k).start()
        side_copy(k).start()
    high_copy.start()

    zero = jnp.zeros((8, a.shape[-1]), jnp.float32)
    for f in range(fields_n):
        for j in range(tiles):
            b[f, HALO - 1, pl.ds(8 * j, 8)] = zero
            b[f, HALO + width, pl.ds(8 * j, 8)] = zero
    plane_copy.wait()
    for s in range(3):
        for f in range(fields_n):
            for j in range(tiles):
                rec[s, f, pl.ds(8 * j, 8)] = 0.05 * rec[s, f, pl.ds(8 * j, 8)]
    low_copy.wait()
    heat_copy.wait()

    row = lax.broadcasted_iota(jnp.int32, zero.shape, 0)
    lane = lax.broadcasted_iota(jnp.int32, zero.shape, 1)
    depth = zero.shape[1]
    first_row = row == 0
    final_row = row == 7
    up = jnp.where(lane == depth - 1, 0.0, 1.0).astype(jnp.float32)
    down = jnp.where(lane == 0, 0.0, 1.0).astype(jnp.float32)
    after = (row < 4) & (gy < last_gy)
    before = (row >= 4) & (gy > 0)
    side_mask = jnp.where(after | before, 1.0, 0.0).astype(jnp.float32)

    def plane_step(old, new, x, slot):
        for j in range(tiles):
            here = pl.ds(8 * j, 8)

            def next_rows(f):
                if j < tiles - 1:
                    return old[f, x, pl.ds(8 * j + 1, 8)]
                return jnp.where(
                    final_row,
                    pltpu.roll(old[f, x, pl.ds(0, 8)], 7, 0),
                    pltpu.roll(old[f, x, here], 7, 0),
                )

            def previous_rows(f):
                if j > 0:
                    return old[f, x, pl.ds(8 * j - 1, 8)]
                return jnp.where(
                    first_row,
                    pltpu.roll(old[f, x, pl.ds(rows, 8)], 1, 0),
                    pltpu.roll(old[f, x, here], 1, 0),
                )

            u = 0.05 * old[2, x, here]
            v = 0.05 * old[3, x, here]
            w = 0.05 * old[4, x, here]
            c_xp, c_xm = 0.02 - u, 0.02 + u
            c_yp, c_ym = 0.02 - v, 0.02 + v
            c_zp, c_zm = up * (0.02 - w), down * (0.02 + w)
            for f in range(fields_n):
                c = old[f, x, here]
                t1 = 0.83 * c + rec[slot, f, here]
                t2 = c_xp * old[f, x + 1, here] + c_xm * old[f, x - 1, here]
                t3 = c_yp * next_rows(f) + c_ym * previous_rows(f)
                t4 = c_zp * pltpu.roll(c, depth - 1, 1) + c_zm * pltpu.roll(c, 1, 1)
                fresh = (t1 + t2) + (t3 + t4)
                if f == 0:
                    fresh = fresh + src[x, here]
                if j == tiles - 1:
                    fresh = fresh * side_mask
                new[f, x, here] = fresh

    for step in range(1, STEPS + 1):
        old, new = (a, b) if step % 2 == 1 else (b, a)
        first = jnp.where(gx == 0, HALO, step)
        end = jnp.where(gx == last_gx, HALO + width, total - step)

        def body(x, carry, old=old, new=new):
            slot = jnp.where(x < HALO, 0, jnp.where(x < HALO + width, 1, 2))
            plane_step(old, new, x, slot)
            return carry

        if step == 1:
            own_copy(0).wait()
            side_copy(0).wait()

            def body1(x, carry):
                ahead = x + 1 - HALO

                @pl.when((ahead > 0) & (ahead < width) & (lax.rem(ahead, CHUNK) == 0))
                def _():
                    k = lax.div(ahead, CHUNK)
                    own_copy(k).wait()
                    side_copy(k).wait()

                @pl.when(ahead == width)
                def _():
                    high_copy.wait()

                slot = jnp.where(x < HALO, 0, jnp.where(x < HALO + width, 1, 2))
                plane_step(a, b, x, slot)
                return carry

            lax.fori_loop(first, end, body1, 0)
        elif step < STEPS:
            lax.fori_loop(first, end, body, 0)
        else:

            def last_body(x, carry, old=old, new=new):
                plane_step(old, new, x, 1)
                done = x + 1 - HALO

                @pl.when(lax.rem(done, CHUNK) == 0)
                def _():
                    out_copy(lax.div(done, CHUNK) - 1).start()

                return carry

            lax.fori_loop(HALO, HALO + width, last_body, 0)
    for k in range(chunks):
        out_copy(k).wait()


def stencil(fields, yside, xlow, xhigh, planes, heat):
    count, width, rows, depth = fields.shape
    total = width + 2 * HALO
    buffer = pltpu.VMEM((count, total, rows + 8, depth), jnp.float32)

    def kernel(fields_, yside_, xlow_, xhigh_, planes_, heat_, out_, a, b, rec, src, in_sems, out_sems):
        stencil_kernel(
            fields_, yside_, xlow_, xhigh_, planes_, heat_, out_, a, b, rec, src, in_sems, out_sems,
            width=width, rows=rows,
        )

    return pl.pallas_call(
        kernel,
        out_shape=jax.ShapeDtypeStruct(fields.shape, jnp.float32),
        in_specs=[pl.BlockSpec(memory_space=pl.ANY)] * 6,
        out_specs=pl.BlockSpec(memory_space=pl.ANY),
        scratch_shapes=[
            buffer,
            buffer,
            pltpu.VMEM((3, count, rows + 8, depth), jnp.float32),
            pltpu.VMEM((total, rows + 8, depth), jnp.float32),
            pltpu.SemaphoreType.DMA((3, max(width // CHUNK, 4))),
            pltpu.SemaphoreType.DMA((width // CHUNK,)),
        ],
        compiler_params=pltpu.CompilerParams(vmem_limit_bytes=48 * 1024 * 1024),
        cost_estimate=pl.CostEstimate(flops=160_000_000, bytes_accessed=20_000_000, transcendentals=0),
        name="stencil",
    )(fields, yside, xlow, xhigh, planes, heat)


def with_sides(cells):
    rows = cells.shape[-2]
    after = shifted(cells[..., :HALO, :], "gy", -1)
    before = shifted(cells[..., rows - HALO :, :], "gy", 1)
    return jnp.concatenate([after, before], axis=-2)


def heating_of(absorbed, face_cell, width, rows, depth):
    flat = face_cell.reshape(-1)
    column = flat // depth
    level = flat % depth
    quarter = depth // 4
    at_column = (column[None, :] == jnp.arange(width * rows, dtype=jnp.int32)[:, None]).astype(jnp.float32)
    at_level = (level[:, None] == jnp.arange(quarter, dtype=jnp.int32)[None, :]).astype(jnp.float32)
    heat = jnp.dot(at_column, at_level * absorbed.reshape(-1)[:, None], precision=HIGH)
    return jnp.pad(heat.reshape(width, rows, quarter), ((0, 0), (0, 0), (0, depth - quarter)))


def local(
    fields,
    emission,
    albedo,
    tile_faces,
    face_cell,
    src_tile,
    dst_tile,
    view_factor,
    pair_count,
    plane_index,
):
    width = fields.shape[1]
    rows = fields.shape[2]
    depth = fields.shape[3]
    n_gx = lax.axis_size("gx")
    n_gy = lax.axis_size("gy")
    pair_slots = src_tile.shape[1]

    yside = with_sides(fields)
    xlow = jnp.concatenate([fields[:, width - HALO :], yside[:, width - HALO :]], axis=2)
    xhigh = jnp.concatenate([fields[:, :HALO], yside[:, :HALO]], axis=2)
    xlow = shifted(xlow, "gx", 1)
    xhigh = shifted(xhigh, "gx", -1)
    plane = jnp.concatenate(
        [
            lax.dynamic_index_in_dim(fields, plane_index[0], 1, keepdims=False),
            lax.dynamic_index_in_dim(yside, plane_index[0], 1, keepdims=False),
        ],
        axis=1,
    )
    plane = shifted(plane, "gx", n_gx // 2, wrap=True)
    planes = jnp.stack([shifted(plane, "gx", 1), plane, shifted(plane, "gx", -1)])

    faces_idx = jnp.arange(FACES, dtype=jnp.int32)
    live = (faces_idx[None, :] < tile_faces[0][:, None]).astype(jnp.float32)
    own_emission = emission[0]
    own_albedo = albedo[0]
    sources = src_tile[0]
    targets = dst_tile[0]
    factors = view_factor[0]
    valid = (jnp.arange(pair_slots, dtype=jnp.int32) < pair_count[0, 0]).astype(jnp.float32)
    dest = targets // TILES_DEV
    onehot_dest = (dest[:, None] == jnp.arange(n_gy, dtype=jnp.int32)[None, :]).astype(
        jnp.int32
    ) * valid.astype(jnp.int32)[:, None]
    before = jnp.cumsum(onehot_dest, axis=0) - onehot_dest
    rank = jnp.sum(before * onehot_dest, axis=1)
    slot = dest * CAP + rank
    slot_idx = jnp.arange(n_gy * CAP, dtype=jnp.int32)
    chosen = (slot[None, :] == slot_idx[:, None]) & (valid[None, :] > 0.5)
    selector = chosen.astype(jnp.float32)
    occupied = jnp.any(chosen, axis=1)
    slot_tile = jnp.sum(jnp.where(chosen, (targets % TILES_DEV)[None, :], 0), axis=1)
    slot_tile = jnp.where(occupied, slot_tile, TILES_DEV)
    arrived_tiles = lax.all_to_all(slot_tile, "gy", split_axis=0, concat_axis=0, tiled=True)
    landing = (arrived_tiles[None, :] == jnp.arange(TILES_DEV, dtype=jnp.int32)[:, None]).astype(
        jnp.float32
    )
    radiosity = live[:, None, :] * own_emission
    incoming = jnp.zeros_like(radiosity)
    for round_idx in range(REFL):
        picked = jnp.take(radiosity, sources, axis=0)
        contrib = jnp.einsum("pij,pbj->pbi", factors, picked, precision=HIGH) * valid[:, None, None]
        outgoing = jnp.einsum("sp,pbi->sbi", selector, contrib, precision=HIGH)
        arrived = lax.all_to_all(outgoing, "gy", split_axis=0, concat_axis=0, tiled=True)
        incoming = jnp.einsum("ts,sbi->tbi", landing, arrived, precision=HIGH)
        radiosity = live[:, None, :] * (own_emission + own_albedo[:, None, :] * incoming)
    absorbed = 0.1 * live * (1.0 - own_albedo) * jnp.sum(incoming, axis=1)
    heat = heating_of(absorbed, face_cell[0], width, rows, depth)
    heat = jnp.concatenate([heat, with_sides(heat)], axis=1)
    heat = jnp.concatenate(
        [shifted(heat[width - HALO :], "gx", 1), heat, shifted(heat[:HALO], "gx", -1)], axis=0
    )
    stepped = stencil(fields, yside, xlow, xhigh, planes, heat)
    return (stepped, radiosity[None])


def solution(mesh):
    return jax.shard_map(
        local,
        mesh=mesh,
        in_specs=(
            P(None, "gx", "gy", None),
            P("gx", "gy", None, None),
            P("gx", "gy", None),
            P("gx", "gy"),
            P("gx", "gy", None),
            P("gx", "gy"),
            P("gx", "gy"),
            P("gx", "gy", None, None),
            P("gx", "gy"),
            P("gx"),
        ),
        out_specs=(P(None, "gx", "gy", None), P("gx", "gy", None, None)),
        check_vma=False,
    )
```

```python
import functools

import jax
import jax.numpy as jnp
from jax import lax
from jax.experimental import pallas as pl
from jax.experimental.pallas import tpu as pltpu
from jax.sharding import PartitionSpec as P

STEPS = 4
TILES_DEV = 16
HALO = STEPS
CHUNK = 8


def shifted(value, axis, steps, wrap=False):
    count = lax.axis_size(axis)
    pairs = [(i, (i + steps) % count) for i in range(count) if wrap or 0 <= i + steps < count]
    return lax.ppermute(value, axis, pairs)


def stencil_kernel(
    fields, yside, xlow, xhigh, plane, heat, hside, hlow, hhigh, out, a, b, rec, src, in_sems, out_sems, *, width, rows
):
    fields_n = fields.shape[0]
    tiles = rows // 8 + 1
    chunks = width // CHUNK
    total = width + 2 * HALO
    gx = lax.axis_index("gx")
    gy = lax.axis_index("gy")
    last_gx = lax.axis_size("gx") - 1
    last_gy = lax.axis_size("gy") - 1

    def own_copy(k):
        return pltpu.make_async_copy(
            fields.at[:, pl.ds(k * CHUNK, CHUNK)],
            a.at[:, pl.ds(HALO + k * CHUNK, CHUNK), pl.ds(0, rows)],
            in_sems.at[0, k],
        )

    def side_copy(k):
        return pltpu.make_async_copy(
            yside.at[:, pl.ds(k * CHUNK, CHUNK)],
            a.at[:, pl.ds(HALO + k * CHUNK, CHUNK), pl.ds(rows, 8)],
            in_sems.at[1, k],
        )

    def out_copy(k):
        return pltpu.make_async_copy(
            a.at[:, pl.ds(HALO + k * CHUNK, CHUNK), pl.ds(0, rows)],
            out.at[:, pl.ds(k * CHUNK, CHUNK)],
            out_sems.at[k],
        )

    low_copy = pltpu.make_async_copy(
        xlow.at[:, pl.ds(0, HALO)], a.at[:, pl.ds(0, HALO)], in_sems.at[2, 0]
    )
    high_copy = pltpu.make_async_copy(
        xhigh.at[:, pl.ds(0, HALO)], a.at[:, pl.ds(HALO + width, HALO)], in_sems.at[2, 1]
    )
    plane_copies = [
        pltpu.make_async_copy(xlow.at[:, HALO], rec.at[0], in_sems.at[2, 2]),
        pltpu.make_async_copy(plane, rec.at[1], in_sems.at[2, 3]),
        pltpu.make_async_copy(xhigh.at[:, HALO], rec.at[2], in_sems.at[2, 4]),
    ]
    block = pl.ds(HALO, width)
    heat_copies = [
        pltpu.make_async_copy(heat, src.at[block, pl.ds(0, rows)], in_sems.at[3, 0]),
        pltpu.make_async_copy(hside, src.at[block, pl.ds(rows, 8)], in_sems.at[3, 1]),
        pltpu.make_async_copy(hlow, src.at[pl.ds(0, HALO)], in_sems.at[3, 2]),
        pltpu.make_async_copy(hhigh, src.at[pl.ds(HALO + width, HALO)], in_sems.at[3, 3]),
    ]
    for copy in plane_copies:
        copy.start()
    low_copy.start()
    for copy in heat_copies:
        copy.start()
    for k in range(chunks):
        own_copy(k).start()
        side_copy(k).start()
    high_copy.start()

    zero = jnp.zeros((8, a.shape[-1]), jnp.float32)
    for f in range(fields_n):
        for j in range(tiles):
            b[f, HALO - 1, pl.ds(8 * j, 8)] = zero
            b[f, HALO + width, pl.ds(8 * j, 8)] = zero
    for copy in plane_copies:
        copy.wait()
    for s in range(3):
        for f in range(fields_n):
            for j in range(tiles):
                rec[s, f, pl.ds(8 * j, 8)] = 0.05 * rec[s, f, pl.ds(8 * j, 8)]
    low_copy.wait()
    for copy in heat_copies:
        copy.wait()

    row = lax.broadcasted_iota(jnp.int32, zero.shape, 0)
    lane = lax.broadcasted_iota(jnp.int32, zero.shape, 1)
    depth = zero.shape[1]
    first_row = row == 0
    final_row = row == 7
    up = jnp.where(lane == depth - 1, 0.0, 1.0).astype(jnp.float32)
    down = jnp.where(lane == 0, 0.0, 1.0).astype(jnp.float32)
    after = (row < 4) & (gy < last_gy)
    before = (row >= 4) & (gy > 0)
    side_mask = jnp.where(after | before, 1.0, 0.0).astype(jnp.float32)

    def plane_step(old, new, x, slot):
        for j in range(tiles):
            here = pl.ds(8 * j, 8)

            def next_rows(f):
                if j < tiles - 1:
                    return old[f, x, pl.ds(8 * j + 1, 8)]
                return jnp.where(
                    final_row,
                    pltpu.roll(old[f, x, pl.ds(0, 8)], 7, 0),
                    pltpu.roll(old[f, x, here], 7, 0),
                )

            def previous_rows(f):
                if j > 0:
                    return old[f, x, pl.ds(8 * j - 1, 8)]
                return jnp.where(
                    first_row,
                    pltpu.roll(old[f, x, pl.ds(rows, 8)], 1, 0),
                    pltpu.roll(old[f, x, here], 1, 0),
                )

            u = 0.05 * old[2, x, here]
            v = 0.05 * old[3, x, here]
            w = 0.05 * old[4, x, here]
            c_xp, c_xm = 0.02 - u, 0.02 + u
            c_yp, c_ym = 0.02 - v, 0.02 + v
            c_zp, c_zm = up * (0.02 - w), down * (0.02 + w)
            for f in range(fields_n):
                c = old[f, x, here]
                t1 = 0.83 * c + rec[slot, f, here]
                t2 = c_xp * old[f, x + 1, here] + c_xm * old[f, x - 1, here]
                t3 = c_yp * next_rows(f) + c_ym * previous_rows(f)
                t4 = c_zp * pltpu.roll(c, depth - 1, 1) + c_zm * pltpu.roll(c, 1, 1)
                fresh = (t1 + t2) + (t3 + t4)
                if f == 0:
                    fresh = fresh + src[x, here]
                if j == tiles - 1:
                    fresh = fresh * side_mask
                new[f, x, here] = fresh

    for step in range(1, STEPS + 1):
        old, new = (a, b) if step % 2 == 1 else (b, a)
        first = jnp.where(gx == 0, HALO, step)
        end = jnp.where(gx == last_gx, HALO + width, total - step)

        def body(x, carry, old=old, new=new):
            slot = jnp.where(x < HALO, 0, jnp.where(x < HALO + width, 1, 2))
            plane_step(old, new, x, slot)
            return carry

        if step == 1:
            own_copy(0).wait()
            side_copy(0).wait()

            def body1(x, carry):
                ahead = x + 1 - HALO

                @pl.when((ahead > 0) & (ahead < width) & (lax.rem(ahead, CHUNK) == 0))
                def _():
                    k = lax.div(ahead, CHUNK)
                    own_copy(k).wait()
                    side_copy(k).wait()

                @pl.when(ahead == width)
                def _():
                    high_copy.wait()

                slot = jnp.where(x < HALO, 0, jnp.where(x < HALO + width, 1, 2))
                plane_step(a, b, x, slot)
                return carry

            lax.fori_loop(first, end, body1, 0)
        elif step < STEPS:
            lax.fori_loop(first, end, body, 0)
        else:

            def last_body(x, carry, old=old, new=new):
                plane_step(old, new, x, 1)
                done = x + 1 - HALO

                @pl.when(lax.rem(done, CHUNK) == 0)
                def _():
                    out_copy(lax.div(done, CHUNK) - 1).start()

                return carry

            lax.fori_loop(HALO, HALO + width, last_body, 0)
    for k in range(chunks):
        out_copy(k).wait()


def stencil(fields, yside, xlow, xhigh, plane, heat, hside, hlow, hhigh):
    count, width, rows, depth = fields.shape
    total = width + 2 * HALO
    buffer = pltpu.VMEM((count, total, rows + 8, depth), jnp.float32)
    return pl.pallas_call(
        functools.partial(stencil_kernel, width=width, rows=rows),
        out_shape=jax.ShapeDtypeStruct(fields.shape, jnp.float32),
        in_specs=[pl.BlockSpec(memory_space=pl.ANY)] * 9,
        out_specs=pl.BlockSpec(memory_space=pl.ANY),
        scratch_shapes=[
            buffer,
            buffer,
            pltpu.VMEM((3, count, rows + 8, depth), jnp.float32),
            pltpu.VMEM((total, rows + 8, depth), jnp.float32),
            pltpu.SemaphoreType.DMA((4, max(width // CHUNK, 5))),
            pltpu.SemaphoreType.DMA((width // CHUNK,)),
        ],
        compiler_params=pltpu.CompilerParams(vmem_limit_bytes=48 * 1024 * 1024),
        cost_estimate=pl.CostEstimate(flops=160_000_000, bytes_accessed=20_000_000, transcendentals=0),
        name="stencil",
    )(fields, yside, xlow, xhigh, plane, heat, hside, hlow, hhigh)


NT = (((1,), (1,)), ((), ()))
PAIR_CHUNK = 8


def split(value):
    high = value.astype(jnp.bfloat16)
    return high, (value - high.astype(jnp.float32)).astype(jnp.bfloat16)


def live_faces(tile_faces, t, shape):
    lane = lax.broadcasted_iota(jnp.int32, shape, 1)
    return jnp.where(lane < tile_faces[0, t], 1.0, 0.0).astype(jnp.float32)


def summed(arrived, t, tiles):
    total = arrived[t]
    for g in range(1, arrived.shape[0] // tiles):
        total = total + arrived[g * tiles + t]
    return total


def flux_kernel(tile_faces, sources, targets, count, emission, albedo, arrived, factors, out, held, lhs, sems):
    tiles, bands, faces = emission.shape
    pairs = factors.shape[0]
    chunks = pairs // PAIR_CHUNK

    def chunk_copy(k):
        part = pl.ds(k * PAIR_CHUNK, PAIR_CHUNK)
        return pltpu.make_async_copy(factors.at[part], held.at[part], sems.at[k])

    for k in range(chunks):
        chunk_copy(k).start()
    out[...] = jnp.zeros_like(out)
    for t in range(tiles):
        radiosity = emission[t]
        if arrived is not None:
            radiosity = radiosity + albedo[pl.ds(t, 1), :] * summed(arrived, t, tiles)
        radiosity = live_faces(tile_faces, t, (bands, faces)) * radiosity
        high, low = split(radiosity)
        high, low = high.astype(jnp.float32), low.astype(jnp.float32)
        nothing = jnp.zeros_like(high)
        left = jnp.concatenate([high, low, nothing, nothing], axis=0)
        right = jnp.concatenate([high, nothing, nothing, nothing], axis=0)
        lhs[t] = jnp.concatenate([left, right], axis=1).astype(jnp.bfloat16)

    def chunk_step(k, carry):
        chunk_copy(k).wait()
        for i in range(PAIR_CHUNK // 2):
            first = k * PAIR_CHUNK + 2 * i
            both = held[pl.ds(first, 2)].reshape(2 * faces, faces)
            rhs = jnp.concatenate(split(both), axis=1)
            rows = jnp.concatenate([lhs[sources[0, first]], lhs[sources[0, first + 1]]], axis=0)
            got = lax.dot_general(rows, rhs, NT, preferred_element_type=jnp.float32)
            for n in range(2):
                part = got[16 * n : 16 * n + 8, n * faces : (n + 1) * faces]
                flux = part[:bands] + part[bands : 2 * bands]
                target = targets[0, first + n]
                out[target] = out[target] + jnp.where(first + n < count[0, 0], flux, 0.0)
        return carry

    lax.fori_loop(0, chunks, chunk_step, 0)


def flux(tile_faces, sources, targets, count, emission, albedo, arrived, factors, slab_tiles):
    tiles, bands, faces = emission.shape
    pairs = factors.shape[0]
    scalar = pl.BlockSpec(memory_space=pltpu.SMEM)
    vector = pl.BlockSpec(memory_space=pltpu.VMEM)
    given = [tile_faces, sources, targets, count, emission, albedo, factors]
    specs = [scalar] * 4 + [vector] * 2 + [pl.BlockSpec(memory_space=pl.ANY)]
    if arrived is None:
        def kernel(a, b, c, d, e, f, factors_, *rest):
            flux_kernel(a, b, c, d, e, f, None, factors_, *rest)
    else:
        given.append(arrived)
        specs.append(vector)

        def kernel(a, b, c, d, e, f, factors_, arrived_, *rest):
            flux_kernel(a, b, c, d, e, f, arrived_, factors_, *rest)

    return pl.pallas_call(
        kernel,
        out_shape=jax.ShapeDtypeStruct((slab_tiles, bands, faces), jnp.float32),
        in_specs=specs,
        out_specs=vector,
        scratch_shapes=[
            pltpu.VMEM(factors.shape, jnp.float32),
            pltpu.VMEM((tiles, 16, 2 * faces), jnp.bfloat16),
            pltpu.SemaphoreType.DMA((pairs // PAIR_CHUNK,)),
        ],
        compiler_params=pltpu.CompilerParams(vmem_limit_bytes=16 * 1024 * 1024),
        cost_estimate=pl.CostEstimate(flops=12_000_000, bytes_accessed=12_000_000, transcendentals=0),
        name="flux",
    )(*given)


def heat_kernel(tile_faces, emission, albedo, cells, arrived, radiosity, heat, low, high, *, width, rows, depth):
    tiles, bands, faces = emission.shape
    quarter = depth // 4
    near = rows // 4
    picks, weights = [], []
    for t in range(tiles):
        live = live_faces(tile_faces, t, (bands, faces))
        incoming = summed(arrived, t, tiles)
        row = albedo[pl.ds(t, 1), :]
        radiosity[t] = live * (emission[t] + row * incoming)
        absorbed = 0.1 * live[:1] * (1.0 - row) * jnp.sum(incoming, axis=0, keepdims=True)
        cell = cells[pl.ds(t, 1), :]
        level = cell & (depth - 1)
        y = (cell >> (depth.bit_length() - 1)) & (rows - 1)
        x = cell >> (depth.bit_length() + rows.bit_length() - 2)
        pick_of = x * near + (y & (near - 1))
        column_of = (y // near) * quarter + level
        at_row = lax.broadcasted_iota(jnp.int32, (width * near, faces), 0) == pick_of
        picks.append(jnp.where(at_row, 1.0, 0.0).astype(jnp.bfloat16))
        at_column = lax.broadcasted_iota(jnp.int32, (4 * quarter, faces), 0) == column_of
        top = absorbed.astype(jnp.bfloat16).astype(jnp.float32)
        weights.append(
            jnp.concatenate(
                [jnp.where(at_column, top, 0.0), jnp.where(at_column, absorbed - top, 0.0)], axis=0
            ).astype(jnp.bfloat16)
        )
    picks = jnp.concatenate(picks, axis=1)
    weights = jnp.concatenate(weights, axis=1)
    got = lax.dot_general(picks, weights, NT, preferred_element_type=jnp.float32)
    got = got[:, :depth] + got[:, depth:]
    lane = lax.broadcasted_iota(jnp.int32, (8, depth), 1)
    for x in range(width):
        for q in range(4):
            for half in range(near // 8):
                block = got[x * near + 8 * half : x * near + 8 * half + 8]
                if q:
                    block = pltpu.roll(block, depth - q * quarter, 1)
                block = jnp.where(lane < quarter, block, 0.0)
                heat[x, pl.ds(q * near + 8 * half, 8)] = block
                if q == 0 and half == 0:
                    low[x] = block[:HALO]
                if q == 3 and half == near // 8 - 1:
                    high[x] = block[8 - HALO :]


def heating(tile_faces, emission, albedo, cells, arrived, width, rows, depth):
    scalar = pl.BlockSpec(memory_space=pltpu.SMEM)
    vector = pl.BlockSpec(memory_space=pltpu.VMEM)
    side = jax.ShapeDtypeStruct((width, HALO, depth), jnp.float32)
    return pl.pallas_call(
        functools.partial(heat_kernel, width=width, rows=rows, depth=depth),
        out_shape=(
            jax.ShapeDtypeStruct(emission.shape, jnp.float32),
            jax.ShapeDtypeStruct((width, rows, depth), jnp.float32),
            side,
            side,
        ),
        in_specs=[scalar] + [vector] * 4,
        out_specs=(vector,) * 4,
        compiler_params=pltpu.CompilerParams(vmem_limit_bytes=24 * 1024 * 1024),
        cost_estimate=pl.CostEstimate(flops=12_000_000, bytes_accessed=4_000_000, transcendentals=0),
        name="heating",
    )(tile_faces, emission, albedo, cells, arrived)


def with_sides(cells):
    rows = cells.shape[-2]
    after = shifted(cells[..., :HALO, :], "gy", -1)
    before = shifted(cells[..., rows - HALO :, :], "gy", 1)
    return jnp.concatenate([after, before], axis=-2)


def local(
    fields,
    emission,
    albedo,
    tile_faces,
    face_cell,
    src_tile,
    dst_tile,
    view_factor,
    pair_count,
    plane_index,
):
    width = fields.shape[1]
    rows = fields.shape[2]
    depth = fields.shape[3]
    n_gx = lax.axis_size("gx")
    n_gy = lax.axis_size("gy")

    yside = with_sides(fields)
    own = emission[0], albedo[0]
    pairs = src_tile, dst_tile, pair_count
    slab_tiles = n_gy * TILES_DEV
    outgoing = flux(tile_faces, *pairs, *own, None, view_factor[0], slab_tiles)
    arrived = lax.all_to_all(outgoing, "gy", split_axis=0, concat_axis=0, tiled=True)

    plane = jnp.concatenate(
        [
            lax.dynamic_index_in_dim(fields, plane_index[0], 1, keepdims=False),
            lax.dynamic_index_in_dim(yside, plane_index[0], 1, keepdims=False),
        ],
        axis=1,
    )
    plane = shifted(plane, "gx", n_gx // 2, wrap=True)

    def slab(start):
        part = slice(start, start + HALO)
        cells = jnp.concatenate([fields[:, part], yside[:, part]], axis=2)
        return jnp.concatenate([cells, plane[:, None]], axis=1)

    xlow = shifted(slab(width - HALO), "gx", 1)
    xhigh = shifted(slab(0), "gx", -1)

    outgoing = flux(tile_faces, *pairs, *own, arrived, view_factor[0], slab_tiles)
    arrived = lax.all_to_all(outgoing, "gy", split_axis=0, concat_axis=0, tiled=True)
    radiosity, heat, low, high = heating(tile_faces, *own, face_cell[0], arrived, width, rows, depth)
    hside = jnp.concatenate([shifted(low, "gy", -1), shifted(high, "gy", 1)], axis=1)
    hends = [jnp.concatenate([heat[p], hside[p]], axis=1) for p in (slice(width - HALO, width), slice(0, HALO))]
    hlow = shifted(hends[0], "gx", 1)
    hhigh = shifted(hends[1], "gx", -1)
    stepped = stencil(fields, yside, xlow, xhigh, plane, heat, hside, hlow, hhigh)
    return (stepped, radiosity[None])


def solution(mesh):
    return jax.shard_map(
        local,
        mesh=mesh,
        in_specs=(
            P(None, "gx", "gy", None),
            P("gx", "gy", None, None),
            P("gx", "gy", None),
            P("gx", "gy"),
            P("gx", "gy", None),
            P("gx", "gy"),
            P("gx", "gy"),
            P("gx", "gy", None, None),
            P("gx", "gy"),
            P("gx"),
        ),
        out_specs=(P(None, "gx", "gy", None), P("gx", "gy", None, None)),
        check_vma=False,
    )
```

```python
import functools

import jax
import jax.numpy as jnp
from jax import lax
from jax.experimental import pallas as pl
from jax.experimental.pallas import tpu as pltpu
from jax.sharding import PartitionSpec as P

STEPS = 4
TILES_DEV = 16
HALO = STEPS
CHUNK = 8
GROUP = 4


def shifted(value, axis, steps, wrap=False):
    count = lax.axis_size(axis)
    pairs = [(i, (i + steps) % count) for i in range(count) if wrap or 0 <= i + steps < count]
    return lax.ppermute(value, axis, pairs)


def stencil_kernel(
    fields, yside, xlow, xhigh, plane, heat, ends, out, a, b, rec, packed, src, in_sems, out_sems, *, width, rows
):
    fields_n = fields.shape[0]
    tiles = rows // 8 + 1
    chunks = width // CHUNK
    total = width + 2 * HALO
    gx = lax.axis_index("gx")
    gy = lax.axis_index("gy")
    last_gx = lax.axis_size("gx") - 1
    last_gy = lax.axis_size("gy") - 1

    def own_copy(k):
        return pltpu.make_async_copy(
            fields.at[:, pl.ds(k * CHUNK, CHUNK)],
            a.at[:, pl.ds(HALO + k * CHUNK, CHUNK), pl.ds(0, rows)],
            in_sems.at[0, k],
        )

    def side_copy(k):
        return pltpu.make_async_copy(
            yside.at[:, pl.ds(k * CHUNK, CHUNK)],
            a.at[:, pl.ds(HALO + k * CHUNK, CHUNK), pl.ds(rows, 8)],
            in_sems.at[1, k],
        )

    def out_copy(k):
        return pltpu.make_async_copy(
            a.at[:, pl.ds(HALO + k * CHUNK, CHUNK), pl.ds(0, rows)],
            out.at[:, pl.ds(k * CHUNK, CHUNK)],
            out_sems.at[k],
        )

    low_copy = pltpu.make_async_copy(
        xlow, a.at[:, pl.ds(0, HALO)], in_sems.at[2, 0]
    )
    high_copy = pltpu.make_async_copy(
        xhigh, a.at[:, pl.ds(HALO + width, HALO)], in_sems.at[2, 1]
    )
    heat_rows = rows // 4 + 8
    near = HALO * heat_rows
    plane_copies = [
        pltpu.make_async_copy(ends.at[0, pl.ds(near, plane.shape[0])], rec.at[0], in_sems.at[2, 2]),
        pltpu.make_async_copy(plane, rec.at[1], in_sems.at[2, 3]),
        pltpu.make_async_copy(ends.at[1, pl.ds(near, plane.shape[0])], rec.at[2], in_sems.at[2, 4]),
    ]
    heat_copies = [
        pltpu.make_async_copy(heat, packed.at[pl.ds(near, width * heat_rows)], in_sems.at[3, 0]),
        pltpu.make_async_copy(ends.at[0, pl.ds(0, near)], packed.at[pl.ds(0, near)], in_sems.at[3, 1]),
        pltpu.make_async_copy(
            ends.at[1, pl.ds(0, near)], packed.at[pl.ds(near + width * heat_rows, near)], in_sems.at[3, 2]
        ),
    ]
    for copy in plane_copies + heat_copies:
        copy.start()
    low_copy.start()
    for k in range(chunks):
        own_copy(k).start()
        side_copy(k).start()
    high_copy.start()

    zero = jnp.zeros((8, a.shape[-1]), jnp.float32)
    for f in range(fields_n):
        for j in range(tiles):
            b[f, HALO - 1, pl.ds(8 * j, 8)] = zero
            b[f, HALO + width, pl.ds(8 * j, 8)] = zero
    row = lax.broadcasted_iota(jnp.int32, zero.shape, 0)
    lane = lax.broadcasted_iota(jnp.int32, zero.shape, 1)
    depth = zero.shape[1]
    for copy in heat_copies:
        copy.wait()

    def unpack(i, carry):
        quarter = depth // 4
        for n in range(CHUNK):
            x = i * CHUNK + n
            for half in range(rows // 32):
                block = packed[pl.ds(x * heat_rows + 8 * half, 8)]
                for q in range(4):
                    part = pltpu.roll(block, depth - q * quarter, 1) if q else block
                    src[x, pl.ds(q * (rows // 4) + 8 * half, 8)] = jnp.where(lane < quarter, part, 0.0)
            src[x, pl.ds(rows, 8)] = packed[pl.ds(x * heat_rows + rows // 4, 8)]
        return carry

    lax.fori_loop(0, total // CHUNK, unpack, 0)
    for copy in plane_copies:
        copy.wait()
    for s in range(3):
        for r in range(fields_n * tiles):
            rec[s, pl.ds(8 * r, 8)] = 0.05 * rec[s, pl.ds(8 * r, 8)]
    low_copy.wait()

    first_row = row == 0
    final_row = row == 7
    up = jnp.where(lane == depth - 1, 0.0, 1.0).astype(jnp.float32)
    down = jnp.where(lane == 0, 0.0, 1.0).astype(jnp.float32)
    after = (row < 4) & (gy < last_gy)
    before = (row >= 4) & (gy > 0)
    side_mask = jnp.where(after | before, 1.0, 0.0).astype(jnp.float32)

    def planes_step(old, new, x, slots, last):
        count = tiles - 1 if last else tiles
        for j in range(count):
            here = pl.ds(8 * j, 8)
            above = pl.ds(8 * ((j + 1) % tiles), 8)
            below = pl.ds(8 * ((j - 1) % tiles), 8)
            columns = [[old[f, x + n, here] for n in range(-1, GROUP + 1)] for f in range(fields_n)]
            for n in range(GROUP):
                at = n + 1
                u = 0.05 * columns[2][at]
                v = 0.05 * columns[3][at]
                w = 0.05 * columns[4][at]
                c_xp, c_xm = 0.02 - u, 0.02 + u
                c_yp, c_ym = 0.02 - v, 0.02 + v
                c_zp, c_zm = up * (0.02 - w), down * (0.02 + w)
                for f in range(fields_n):
                    c = columns[f][at]
                    if j < tiles - 1:
                        yp = old[f, x + n, pl.ds(8 * j + 1, 8)]
                    else:
                        yp = jnp.where(final_row, pltpu.roll(old[f, x + n, above], 7, 0), pltpu.roll(c, 7, 0))
                    if j > 0:
                        ym = old[f, x + n, pl.ds(8 * j - 1, 8)]
                    else:
                        ym = jnp.where(first_row, pltpu.roll(old[f, x + n, below], 1, 0), pltpu.roll(c, 1, 0))
                    t1 = 0.83 * c + rec[slots[n], pl.ds(8 * (f * tiles + j), 8)]
                    t2 = c_xp * columns[f][at + 1] + c_xm * columns[f][at - 1]
                    t3 = c_yp * yp + c_ym * ym
                    t4 = c_zp * pltpu.roll(c, depth - 1, 1) + c_zm * pltpu.roll(c, 1, 1)
                    value = (t1 + t2) + (t3 + t4)
                    if f == 0:
                        value = value + src[x + n, here]
                    if j == tiles - 1:
                        value = value * side_mask
                    new[f, x + n, here] = value

    own_copy(0).wait()
    side_copy(0).wait()
    for step in range(1, STEPS + 1):
        old, new = (a, b) if step % 2 == 1 else (b, a)
        first = jnp.where(gx == 0, HALO, step)
        end = jnp.where(gx == last_gx, HALO + width, total - step)

        def body(i, carry, old=old, new=new, step=step, first=first, end=end):
            x = jnp.minimum(first + GROUP * i, end - GROUP)
            if step == 1:
                part = lax.div(x + GROUP - HALO + CHUNK, CHUNK) - 1
                past = lax.div(first + GROUP * i - HALO + CHUNK, CHUNK) - 1

                @pl.when((part > past) & (part > 0) & (part < chunks))
                def _():
                    own_copy(part).wait()
                    side_copy(part).wait()

                @pl.when((part > past) & (part == chunks))
                def _():
                    high_copy.wait()

            def slot(n):
                if step == STEPS:
                    return 1
                return jnp.where(x + n < HALO, 0, jnp.where(x + n < HALO + width, 1, 2))

            planes_step(old, new, x, [slot(n) for n in range(GROUP)], step == STEPS)
            if step == STEPS:
                done = x + GROUP - HALO

                @pl.when(lax.rem(done, CHUNK) == 0)
                def _():
                    out_copy(lax.div(done, CHUNK) - 1).start()

            return carry

        lax.fori_loop(0, lax.div(end - first + GROUP - 1, GROUP), body, 0)
    for k in range(chunks):
        out_copy(k).wait()


def stencil(fields, yside, xlow, xhigh, plane, heat, ends):
    count, width, rows, depth = fields.shape
    total = width + 2 * HALO
    buffer = pltpu.VMEM((count, total, rows + 8, depth), jnp.float32)
    return pl.pallas_call(
        functools.partial(stencil_kernel, width=width, rows=rows),
        out_shape=jax.ShapeDtypeStruct(fields.shape, jnp.float32),
        in_specs=[pl.BlockSpec(memory_space=pl.ANY)] * 7,
        out_specs=pl.BlockSpec(memory_space=pl.ANY),
        scratch_shapes=[
            buffer,
            buffer,
            pltpu.VMEM((3, count * (rows + 8), depth), jnp.float32),
            pltpu.VMEM((total * (rows // 4 + 8), depth), jnp.float32),
            pltpu.VMEM((total, rows + 8, depth), jnp.float32),
            pltpu.SemaphoreType.DMA((4, max(width // CHUNK, 5))),
            pltpu.SemaphoreType.DMA((width // CHUNK,)),
        ],
        compiler_params=pltpu.CompilerParams(vmem_limit_bytes=48 * 1024 * 1024),
        cost_estimate=pl.CostEstimate(flops=160_000_000, bytes_accessed=20_000_000, transcendentals=0),
        name="stencil",
    )(fields, yside, xlow, xhigh, plane, heat, ends)


NT = (((1,), (1,)), ((), ()))
PAIR_CHUNK = 8


def split(value):
    high = value.astype(jnp.bfloat16)
    return high, (value - high.astype(jnp.float32)).astype(jnp.bfloat16)


def live_faces(counts, t, shape):
    lane = lax.broadcasted_iota(jnp.int32, shape, 1)
    return jnp.where(lane < counts[0, t], 1.0, 0.0).astype(jnp.float32)


def summed(arrived, block, blocks):
    total = arrived[block]
    for g in range(1, arrived.shape[0] // blocks):
        total = total + arrived[g * blocks + block]
    return total


def flux_kernel(counts, emission, albedo, factors, *rest, devices, last):
    arrived, (out, held, lhs, sems) = (rest[0] if last else None), rest[-4:]
    tiles, bands, faces = emission.shape
    pairs = factors.shape[0]
    chunks = pairs // PAIR_CHUNK
    blocks = out.shape[0] // devices

    def chunk_copy(k):
        part = pl.ds(k * PAIR_CHUNK, PAIR_CHUNK)
        return pltpu.make_async_copy(factors.at[part], held.at[part], sems.at[k])

    for k in range(chunks):
        chunk_copy(k).start()
    out[...] = jnp.zeros_like(out)
    for t in range(tiles):
        radiosity = emission[t]
        if last:
            radiosity = radiosity + albedo[pl.ds(t, 1), :] * summed(arrived, t, tiles)
        radiosity = live_faces(counts, t, (bands, faces)) * radiosity
        high, low = split(radiosity)
        high, low = high.astype(jnp.float32), low.astype(jnp.float32)
        nothing = jnp.zeros_like(high)
        left = jnp.concatenate([high, low, nothing, nothing], axis=0)
        right = jnp.concatenate([high, nothing, nothing, nothing], axis=0)
        lhs[t] = jnp.concatenate([left, right], axis=1).astype(jnp.bfloat16)

    def chunk_step(k, carry):
        chunk_copy(k).wait()
        for i in range(PAIR_CHUNK // 2):
            first = k * PAIR_CHUNK + 2 * i
            both = held[pl.ds(first, 2)].reshape(2 * faces, faces)
            rhs = jnp.concatenate(split(both), axis=1)
            rows = [lhs[counts[0, tiles + first + n]] for n in range(2)]
            got = lax.dot_general(jnp.concatenate(rows, axis=0), rhs, NT, preferred_element_type=jnp.float32)
            for n in range(2):
                part = got[16 * n : 16 * n + 8, n * faces : (n + 1) * faces]
                flux = part[:bands] + part[bands : 2 * bands]
                target = counts[0, tiles + pairs + first + n]
                if last:
                    target = lax.div(target, tiles) * blocks + lax.rem(target, tiles)
                out[target] = out[target] + jnp.where(first + n < counts[0, tiles + 2 * pairs], flux, 0.0)
        return carry

    lax.fori_loop(0, chunks, chunk_step, 0)
    if last:
        groups = tiles // bands
        for e in range(devices):
            for q in range(groups):
                sums = [
                    jnp.sum(out[e * blocks + q * bands + n], axis=0, keepdims=True) for n in range(bands)
                ]
                sums = jnp.concatenate(sums, axis=0)
                if e + 1 < devices:
                    out[(e + 1) * blocks + tiles + q] = sums
                if e > 0:
                    out[(e - 1) * blocks + tiles + groups + q] = sums


def flux(counts, emission, albedo, factors, devices, arrived=None):
    tiles, bands, faces = emission.shape
    pairs = factors.shape[0]
    last = arrived is not None
    blocks = tiles + (2 * tiles // bands if last else 0)
    vector = pl.BlockSpec(memory_space=pltpu.VMEM)
    return pl.pallas_call(
        functools.partial(flux_kernel, devices=devices, last=last),
        out_shape=jax.ShapeDtypeStruct((devices * blocks, bands, faces), jnp.float32),
        in_specs=[pl.BlockSpec(memory_space=pltpu.SMEM), vector, vector, pl.BlockSpec(memory_space=pl.ANY)]
        + [vector] * last,
        out_specs=vector,
        scratch_shapes=[
            pltpu.VMEM(factors.shape, jnp.float32),
            pltpu.VMEM((tiles, 16, 2 * faces), jnp.bfloat16),
            pltpu.SemaphoreType.DMA((pairs // PAIR_CHUNK,)),
        ],
        compiler_params=pltpu.CompilerParams(vmem_limit_bytes=60 * 1024 * 1024),
        cost_estimate=pl.CostEstimate(flops=1000, bytes_accessed=1000, transcendentals=0),
        name="flux",
    )(counts, emission, albedo, factors, *([arrived] if last else []))


def one_hot(count, index):
    at = lax.broadcasted_iota(jnp.int32, (count, index.shape[1]), 0) == index
    return at


def weighed(count, index, value):
    at = one_hot(count, index)
    top = value.astype(jnp.bfloat16).astype(jnp.float32)
    both = [jnp.where(at, top, 0.0), jnp.where(at, value - top, 0.0)]
    return jnp.concatenate(both, axis=0).astype(jnp.bfloat16)


def picked(count, index):
    return jnp.where(one_hot(count, index), 1.0, 0.0).astype(jnp.bfloat16)


def heat_kernel(
    counts, emission, albedo, cells, after, before, arrived, radiosity, heat, *, width, rows, depth
):
    tiles, bands, faces = emission.shape
    quarter = depth // 4
    near = rows // 4
    blocks = tiles + 2 * tiles // bands
    level_bits = depth.bit_length() - 1
    row_bits = rows.bit_length() - 1

    def place(cell):
        return cell >> (level_bits + row_bits), (cell >> level_bits) & (rows - 1), cell & (depth - 1)

    picks, weights = [], []
    for t in range(tiles):
        live = live_faces(counts, t, (bands, faces))
        incoming = summed(arrived, t, blocks)
        share = albedo[pl.ds(t, 1), :]
        radiosity[t] = live * (emission[t] + share * incoming)
        absorbed = 0.1 * live[:1] * (1.0 - share) * jnp.sum(incoming, axis=0, keepdims=True)
        x, y, level = place(cells[pl.ds(t, 1), :])
        picks.append(picked(width * near, x * near + (y & (near - 1))))
        weights.append(weighed(depth, (y // near) * quarter + level, absorbed))
    got = lax.dot_general(
        jnp.concatenate(picks, axis=1), jnp.concatenate(weights, axis=1), NT, preferred_element_type=jnp.float32
    )
    got = got[:, :depth] + got[:, depth:]

    picks, weights = [], []
    groups = tiles // bands
    for side, about in enumerate((before, after)):
        for q in range(groups):
            incoming = summed(arrived, tiles + side * groups + q, blocks)
            absorbed = about[q] * incoming
            cell = about[groups + q].astype(jnp.int32)
            for n in range(bands):
                x, y, level = place(cell[n : n + 1])
                if side:
                    row = jnp.where(y < HALO, x * 8 + y, -1)
                else:
                    row = jnp.where(y >= rows - HALO, x * 8 + HALO + y - (rows - HALO), -1)
                picks.append(picked(width * 8, row))
                weights.append(weighed(quarter, level, absorbed[n : n + 1]))
    sides = lax.dot_general(
        jnp.concatenate(picks, axis=1), jnp.concatenate(weights, axis=1), NT, preferred_element_type=jnp.float32
    )
    sides = sides[:, :quarter] + sides[:, quarter:]
    sides = jnp.concatenate([sides, jnp.zeros((width * 8, depth - quarter), jnp.float32)], axis=1)
    for x in range(width):
        heat[pl.ds(x * (near + 8), near)] = got[x * near : (x + 1) * near]
        heat[pl.ds(x * (near + 8) + near, 8)] = sides[8 * x : 8 * x + 8]


def heating(counts, emission, albedo, cells, after, before, arrived, width, rows, depth):
    vector = pl.BlockSpec(memory_space=pltpu.VMEM)
    return pl.pallas_call(
        functools.partial(heat_kernel, width=width, rows=rows, depth=depth),
        out_shape=(
            jax.ShapeDtypeStruct(emission.shape, jnp.float32),
            jax.ShapeDtypeStruct((width * (rows // 4 + 8), depth), jnp.float32),
        ),
        in_specs=[pl.BlockSpec(memory_space=pltpu.SMEM)] + [vector] * 6,
        out_specs=(vector,) * 2,
        compiler_params=pltpu.CompilerParams(vmem_limit_bytes=32 * 1024 * 1024),
        cost_estimate=pl.CostEstimate(flops=1000, bytes_accessed=1000, transcendentals=0),
        name="heating",
    )(counts, emission, albedo, cells, after, before, arrived)


def local(
    fields,
    emission,
    albedo,
    tile_faces,
    face_cell,
    src_tile,
    dst_tile,
    view_factor,
    pair_count,
    plane_index,
):
    width = fields.shape[1]
    rows = fields.shape[2]
    depth = fields.shape[3]
    n_gx = lax.axis_size("gx")
    n_gy = lax.axis_size("gy")

    counts = jnp.concatenate([tile_faces, src_tile, dst_tile, pair_count], axis=1)
    own = counts, emission[0], albedo[0]
    bands, faces = emission.shape[2:]
    live = (jnp.arange(faces, dtype=jnp.int32) < tile_faces[0][:, None]).astype(jnp.float32)
    about = jnp.concatenate([0.1 * live * (1.0 - albedo[0]), face_cell[0].astype(jnp.float32)], axis=0)
    about = about.reshape(-1, HALO, faces)

    def side(start):
        edge = fields[:, :, start : start + HALO].reshape(-1, HALO, depth)
        return jnp.concatenate([edge, about], axis=0)

    after = shifted(side(0), "gy", -1)
    before = shifted(side(rows - HALO), "gy", 1)
    count = fields.shape[0] * width
    yside = jnp.concatenate([after[:count], before[:count]], axis=1).reshape(-1, width, 2 * HALO, depth)
    about = after[count:], before[count:]

    outgoing = flux(*own, view_factor[0], n_gy)
    arrived = lax.all_to_all(outgoing, "gy", split_axis=0, concat_axis=0, tiled=True)

    def slab(start):
        part = slice(start, start + HALO)
        return jnp.concatenate([fields[:, part], yside[:, part]], axis=2)

    plane = jnp.concatenate(
        [
            lax.dynamic_index_in_dim(fields, plane_index[0], 1, keepdims=False),
            lax.dynamic_index_in_dim(yside, plane_index[0], 1, keepdims=False),
        ],
        axis=1,
    )
    low, high = slab(0), slab(width - HALO)
    arrived, plane, low, high = lax.optimization_barrier((arrived, plane, low, high))
    plane = shifted(plane, "gx", n_gx // 2, wrap=True).reshape(-1, depth)
    xlow = shifted(high, "gx", 1)
    xhigh = shifted(low, "gx", -1)

    outgoing = flux(*own, view_factor[0], n_gy, arrived)
    outgoing, plane = lax.optimization_barrier((outgoing, plane))
    arrived = lax.all_to_all(outgoing, "gy", split_axis=0, concat_axis=0, tiled=True)
    radiosity, heat = heating(*own, face_cell[0], *about, arrived, width, rows, depth)
    near = HALO * (rows // 4 + 8)
    ends = jnp.stack(
        [
            shifted(jnp.concatenate([heat[heat.shape[0] - near :], plane], axis=0), "gx", 1),
            shifted(jnp.concatenate([heat[:near], plane], axis=0), "gx", -1),
        ]
    )
    stepped = stencil(fields, yside, xlow, xhigh, plane, heat, ends)
    return (stepped, radiosity[None])


def solution(mesh):
    return jax.shard_map(
        local,
        mesh=mesh,
        in_specs=(
            P(None, "gx", "gy", None),
            P("gx", "gy", None, None),
            P("gx", "gy", None),
            P("gx", "gy"),
            P("gx", "gy", None),
            P("gx", "gy"),
            P("gx", "gy"),
            P("gx", "gy", None, None),
            P("gx", "gy"),
            P("gx"),
        ),
        out_specs=(P(None, "gx", "gy", None), P("gx", "gy", None, None)),
        check_vma=False,
    )
```

```python
import functools

import jax
import jax.numpy as jnp
from jax import lax
from jax.experimental import pallas as pl
from jax.experimental.pallas import tpu as pltpu
from jax.sharding import PartitionSpec as P

STEPS = 4
HALO = STEPS
CHUNK = 8
GROUP = 4


def shifted(value, axis, steps, wrap=False):
    count = lax.axis_size(axis)
    pairs = [(i, (i + steps) % count) for i in range(count) if wrap or 0 <= i + steps < count]
    return lax.ppermute(value, axis, pairs)


def stencil_kernel(
    fields, yside, xlow, xhigh, plane, relay_low, relay_high, heat, end_low, end_high, out,
    a, b, rec, packed, src, in_sems, out_sems, *, width, rows
):
    fields_n = fields.shape[0]
    tiles = rows // 8 + 1
    chunks = width // CHUNK
    total = width + 2 * HALO
    gx = lax.axis_index("gx")
    gy = lax.axis_index("gy")
    last_gx = lax.axis_size("gx") - 1
    last_gy = lax.axis_size("gy") - 1

    def own_copy(k):
        return pltpu.make_async_copy(
            fields.at[:, pl.ds(k * CHUNK, CHUNK)],
            a.at[:, pl.ds(HALO + k * CHUNK, CHUNK), pl.ds(0, rows)],
            in_sems.at[0, k],
        )

    def side_copy(k):
        return pltpu.make_async_copy(
            yside.at[:, pl.ds(k * CHUNK, CHUNK)],
            a.at[:, pl.ds(HALO + k * CHUNK, CHUNK), pl.ds(rows, 8)],
            in_sems.at[1, k],
        )

    def out_copy(k):
        return pltpu.make_async_copy(
            a.at[:, pl.ds(HALO + k * CHUNK, CHUNK), pl.ds(0, rows)],
            out.at[:, pl.ds(k * CHUNK, CHUNK)],
            out_sems.at[k],
        )

    low_copy = pltpu.make_async_copy(
        xlow, a.at[:, pl.ds(0, HALO)], in_sems.at[2, 0]
    )
    high_copy = pltpu.make_async_copy(
        xhigh, a.at[:, pl.ds(HALO + width, HALO)], in_sems.at[2, 1]
    )
    heat_rows = rows // 4 + 8
    near = HALO * heat_rows
    plane_copies = [
        pltpu.make_async_copy(relay_low, rec.at[0], in_sems.at[2, 2]),
        pltpu.make_async_copy(plane, rec.at[1], in_sems.at[2, 3]),
        pltpu.make_async_copy(relay_high, rec.at[2], in_sems.at[2, 4]),
    ]
    heat_copies = [
        pltpu.make_async_copy(heat, packed.at[pl.ds(near, width * heat_rows)], in_sems.at[3, 0]),
        pltpu.make_async_copy(end_low, packed.at[pl.ds(0, near)], in_sems.at[3, 1]),
        pltpu.make_async_copy(
            end_high, packed.at[pl.ds(near + width * heat_rows, near)], in_sems.at[3, 2]
        ),
    ]
    for copy in heat_copies + plane_copies:
        copy.start()
    low_copy.start()
    for k in range(chunks):
        own_copy(k).start()
        side_copy(k).start()
    high_copy.start()

    zero = jnp.zeros((8, a.shape[-1]), jnp.float32)
    for f in range(fields_n):
        for j in range(tiles):
            b[f, HALO - 1, pl.ds(8 * j, 8)] = zero
            b[f, HALO + width, pl.ds(8 * j, 8)] = zero
    row = lax.broadcasted_iota(jnp.int32, zero.shape, 0)
    lane = lax.broadcasted_iota(jnp.int32, zero.shape, 1)
    depth = zero.shape[1]
    for copy in heat_copies:
        copy.wait()

    def unpack(i, carry):
        quarter = depth // 4
        for n in range(CHUNK):
            x = i * CHUNK + n
            for half in range(rows // 32):
                block = packed[pl.ds(x * heat_rows + 8 * half, 8)]
                for q in range(4):
                    part = pltpu.roll(block, depth - q * quarter, 1) if q else block
                    src[x, pl.ds(q * (rows // 4) + 8 * half, 8)] = jnp.where(lane < quarter, part, 0.0)
            src[x, pl.ds(rows, 8)] = packed[pl.ds(x * heat_rows + rows // 4, 8)]
        return carry

    lax.fori_loop(0, total // CHUNK, unpack, 0)
    for copy in plane_copies:
        copy.wait()
    for s in range(3):
        for r in range(fields_n * tiles):
            rec[s, pl.ds(8 * r, 8)] = 0.05 * rec[s, pl.ds(8 * r, 8)]
    low_copy.wait()

    first_row = row == 0
    final_row = row == 7
    up = jnp.where(lane == depth - 1, 0.0, 1.0).astype(jnp.float32)
    down = jnp.where(lane == 0, 0.0, 1.0).astype(jnp.float32)
    after = (row < 4) & (gy < last_gy)
    before = (row >= 4) & (gy > 0)
    side_mask = jnp.where(after | before, 1.0, 0.0).astype(jnp.float32)

    def planes_step(old, new, x, slots, last):
        count = tiles - 1 if last else tiles
        for j in range(count):
            here = pl.ds(8 * j, 8)
            above = pl.ds(8 * ((j + 1) % tiles), 8)
            below = pl.ds(8 * ((j - 1) % tiles), 8)
            columns = [[old[f, x + n, here] for n in range(-1, GROUP + 1)] for f in range(fields_n)]
            for n in range(GROUP):
                at = n + 1
                u = 0.05 * columns[2][at]
                v = 0.05 * columns[3][at]
                w = 0.05 * columns[4][at]
                c_xp, c_xm = 0.02 - u, 0.02 + u
                c_yp, c_ym = 0.02 - v, 0.02 + v
                c_zp, c_zm = up * (0.02 - w), down * (0.02 + w)
                for f in range(fields_n):
                    c = columns[f][at]
                    if j < tiles - 1:
                        yp = old[f, x + n, pl.ds(8 * j + 1, 8)]
                    else:
                        yp = jnp.where(final_row, pltpu.roll(old[f, x + n, above], 7, 0), pltpu.roll(c, 7, 0))
                    if j > 0:
                        ym = old[f, x + n, pl.ds(8 * j - 1, 8)]
                    else:
                        ym = jnp.where(first_row, pltpu.roll(old[f, x + n, below], 1, 0), pltpu.roll(c, 1, 0))
                    t1 = 0.83 * c + rec[slots[n], pl.ds(8 * (f * tiles + j), 8)]
                    t2 = c_xp * columns[f][at + 1] + c_xm * columns[f][at - 1]
                    t3 = c_yp * yp + c_ym * ym
                    t4 = c_zp * pltpu.roll(c, depth - 1, 1) + c_zm * pltpu.roll(c, 1, 1)
                    value = (t1 + t2) + (t3 + t4)
                    if f == 0:
                        value = value + src[x + n, here]
                    if j == tiles - 1:
                        value = value * side_mask
                    new[f, x + n, here] = value

    own_copy(0).wait()
    side_copy(0).wait()
    for step in range(1, STEPS + 1):
        old, new = (a, b) if step % 2 == 1 else (b, a)
        first = jnp.where(gx == 0, HALO, step)
        end = jnp.where(gx == last_gx, HALO + width, total - step)

        def body(i, carry, old=old, new=new, step=step, first=first, end=end):
            x = jnp.minimum(first + GROUP * i, end - GROUP)
            if step == 1:
                part = lax.div(x + GROUP - HALO + CHUNK, CHUNK) - 1
                past = lax.div(first + GROUP * i - HALO + CHUNK, CHUNK) - 1

                @pl.when((part > past) & (part > 0) & (part < chunks))
                def _():
                    own_copy(part).wait()
                    side_copy(part).wait()

                @pl.when((part > past) & (part == chunks))
                def _():
                    high_copy.wait()

            def slot(n):
                if step == STEPS:
                    return 1
                return jnp.where(x + n < HALO, 0, jnp.where(x + n < HALO + width, 1, 2))

            planes_step(old, new, x, [slot(n) for n in range(GROUP)], step == STEPS)
            if step == STEPS:
                done = x + GROUP - HALO

                @pl.when(lax.rem(done, CHUNK) == 0)
                def _():
                    out_copy(lax.div(done, CHUNK) - 1).start()

            return carry

        lax.fori_loop(0, lax.div(end - first + GROUP - 1, GROUP), body, 0)
    for k in range(chunks):
        out_copy(k).wait()


def stencil(fields, *others):
    count, width, rows, depth = fields.shape
    total = width + 2 * HALO
    buffer = pltpu.VMEM((count, total, rows + 8, depth), jnp.float32)
    return pl.pallas_call(
        functools.partial(stencil_kernel, width=width, rows=rows),
        out_shape=jax.ShapeDtypeStruct(fields.shape, jnp.float32),
        in_specs=[pl.BlockSpec(memory_space=pl.ANY)] * 10,
        out_specs=pl.BlockSpec(memory_space=pl.ANY),
        scratch_shapes=[
            buffer,
            buffer,
            pltpu.VMEM((3, count * (rows + 8), depth), jnp.float32),
            pltpu.VMEM((total * (rows // 4 + 8), depth), jnp.float32),
            pltpu.VMEM((total, rows + 8, depth), jnp.float32),
            pltpu.SemaphoreType.DMA((4, max(width // CHUNK, 5))),
            pltpu.SemaphoreType.DMA((width // CHUNK,)),
        ],
        compiler_params=pltpu.CompilerParams(vmem_limit_bytes=48 * 1024 * 1024),
        cost_estimate=pl.CostEstimate(flops=160_000_000, bytes_accessed=20_000_000, transcendentals=0),
        name="stencil",
    )(fields, *others)


NT = (((1,), (1,)), ((), ()))
PAIR_CHUNK = 8


def split(value):
    high = value.astype(jnp.bfloat16)
    return high, (value - high.astype(jnp.float32)).astype(jnp.bfloat16)


def live_faces(counts, t, shape):
    lane = lax.broadcasted_iota(jnp.int32, shape, 1)
    return jnp.where(lane < counts[0, t], 1.0, 0.0).astype(jnp.float32)


def summed(arrived, block, blocks):
    total = arrived[block]
    for g in range(1, arrived.shape[0] // blocks):
        total = total + arrived[g * blocks + block]
    return total


def fetched(arrays, scratch, sems):
    copies = [pltpu.make_async_copy(a, s, sems.at[n]) for n, (a, s) in enumerate(zip(arrays, scratch))]
    for copy in copies:
        copy.start()
    return copies


def flux_kernel(tile_faces, sources, targets, count, emission, albedo, factors, *rest, devices, last):
    arrived, (out, held, lhs, *integers, int_sems, sems) = (rest[0] if last else None), rest[last:]
    tiles, bands, faces = emission.shape
    pairs = factors.shape[0]
    chunks = pairs // PAIR_CHUNK
    blocks = out.shape[0] // devices

    def chunk_copy(k):
        part = pl.ds(k * PAIR_CHUNK, PAIR_CHUNK)
        return pltpu.make_async_copy(factors.at[part], held.at[part], sems.at[k])

    copies = fetched((tile_faces, sources, targets, count), integers, int_sems)
    for k in range(chunks):
        chunk_copy(k).start()
    out[...] = jnp.zeros_like(out)
    for copy in copies:
        copy.wait()
    tile_faces, sources, targets, count = integers
    for t in range(tiles):
        radiosity = emission[t]
        if last:
            radiosity = radiosity + albedo[pl.ds(t, 1), :] * summed(arrived, t, tiles)
        radiosity = live_faces(tile_faces, t, (bands, faces)) * radiosity
        high, low = split(radiosity)
        high, low = high.astype(jnp.float32), low.astype(jnp.float32)
        nothing = jnp.zeros_like(high)
        left = jnp.concatenate([high, low, nothing, nothing], axis=0)
        right = jnp.concatenate([high, nothing, nothing, nothing], axis=0)
        lhs[t] = jnp.concatenate([left, right], axis=1).astype(jnp.bfloat16)

    def chunk_step(k, carry):
        chunk_copy(k).wait()
        for i in range(PAIR_CHUNK // 2):
            first = k * PAIR_CHUNK + 2 * i
            both = held[pl.ds(first, 2)].reshape(2 * faces, faces)
            rhs = jnp.concatenate(split(both), axis=1)
            rows = [lhs[sources[0, first + n]] for n in range(2)]
            got = lax.dot_general(jnp.concatenate(rows, axis=0), rhs, NT, preferred_element_type=jnp.float32)
            for n in range(2):
                part = got[16 * n : 16 * n + 8, n * faces : (n + 1) * faces]
                flux = part[:bands] + part[bands : 2 * bands]
                target = targets[0, first + n]
                if last:
                    target = lax.div(target, tiles) * blocks + lax.rem(target, tiles)
                out[target] = out[target] + jnp.where(first + n < count[0, 0], flux, 0.0)
        return carry

    lax.fori_loop(0, chunks, chunk_step, 0)
    if last:
        groups = tiles // bands
        for e in range(devices):
            for q in range(groups):
                sums = [
                    jnp.sum(out[e * blocks + q * bands + n], axis=0, keepdims=True) for n in range(bands)
                ]
                sums = jnp.concatenate(sums, axis=0)
                if e + 1 < devices:
                    out[(e + 1) * blocks + tiles + q] = sums
                if e > 0:
                    out[(e - 1) * blocks + tiles + groups + q] = sums


def flux(integers, emission, albedo, factors, devices, arrived=None):
    tiles, bands, faces = emission.shape
    pairs = factors.shape[0]
    last = arrived is not None
    blocks = tiles + (2 * tiles // bands if last else 0)
    vector = pl.BlockSpec(memory_space=pltpu.VMEM)
    anywhere = pl.BlockSpec(memory_space=pl.ANY)
    return pl.pallas_call(
        functools.partial(flux_kernel, devices=devices, last=last),
        out_shape=jax.ShapeDtypeStruct((devices * blocks, bands, faces), jnp.float32),
        in_specs=[anywhere] * 4 + [vector, vector, anywhere] + [vector] * last,
        out_specs=vector,
        scratch_shapes=[
            pltpu.VMEM(factors.shape, jnp.float32),
            pltpu.VMEM((tiles, 16, 2 * faces), jnp.bfloat16),
            *[pltpu.SMEM(a.shape, jnp.int32) for a in integers],
            pltpu.SemaphoreType.DMA((len(integers),)),
            pltpu.SemaphoreType.DMA((pairs // PAIR_CHUNK,)),
        ],
        compiler_params=pltpu.CompilerParams(vmem_limit_bytes=60 * 1024 * 1024),
        cost_estimate=pl.CostEstimate(flops=1000, bytes_accessed=1000, transcendentals=0),
        name="flux",
    )(*integers, emission, albedo, factors, *([arrived] if last else []))


def one_hot(count, index):
    at = lax.broadcasted_iota(jnp.int32, (count, index.shape[1]), 0) == index
    return at


def weighed(count, index, value):
    at = one_hot(count, index)
    top = value.astype(jnp.bfloat16).astype(jnp.float32)
    both = [jnp.where(at, top, 0.0), jnp.where(at, value - top, 0.0)]
    return jnp.concatenate(both, axis=0).astype(jnp.bfloat16)


def picked(count, index):
    return jnp.where(one_hot(count, index), 1.0, 0.0).astype(jnp.bfloat16)


def heat_kernel(
    tile_faces, emission, albedo, cells, about, arrived, radiosity, heat, integers, int_sems, *, width, rows, depth
):
    tiles, bands, faces = emission.shape
    quarter = depth // 4
    near = rows // 4
    blocks = tiles + 2 * tiles // bands
    level_bits = depth.bit_length() - 1
    row_bits = rows.bit_length() - 1

    fetched((tile_faces,), (integers,), int_sems)[0].wait()
    tile_faces = integers

    def place(cell):
        return cell >> (level_bits + row_bits), (cell >> level_bits) & (rows - 1), cell & (depth - 1)

    picks, weights = [], []
    for t in range(tiles):
        live = live_faces(tile_faces, t, (bands, faces))
        incoming = summed(arrived, t, blocks)
        share = albedo[pl.ds(t, 1), :]
        radiosity[t] = live * (emission[t] + share * incoming)
        absorbed = 0.1 * live[:1] * (1.0 - share) * jnp.sum(incoming, axis=0, keepdims=True)
        x, y, level = place(cells[pl.ds(t, 1), :])
        picks.append(picked(width * near, x * near + (y & (near - 1))))
        weights.append(weighed(depth, (y // near) * quarter + level, absorbed))
    got = lax.dot_general(
        jnp.concatenate(picks, axis=1), jnp.concatenate(weights, axis=1), NT, preferred_element_type=jnp.float32
    )
    got = got[:, :depth] + got[:, depth:]

    picks, weights = [], []
    groups = tiles // bands
    for side in range(2):
        for q in range(groups):
            incoming = summed(arrived, tiles + side * groups + q, blocks)
            absorbed = about[side, q] * incoming
            cell = about[side, groups + q].astype(jnp.int32)
            for n in range(bands):
                x, y, level = place(cell[n : n + 1])
                if side:
                    row = jnp.where(y < HALO, x * 8 + y, -1)
                else:
                    row = jnp.where(y >= rows - HALO, x * 8 + HALO + y - (rows - HALO), -1)
                picks.append(picked(width * 8, row))
                weights.append(weighed(quarter, level, absorbed[n : n + 1]))
    sides = lax.dot_general(
        jnp.concatenate(picks, axis=1), jnp.concatenate(weights, axis=1), NT, preferred_element_type=jnp.float32
    )
    sides = sides[:, :quarter] + sides[:, quarter:]
    sides = jnp.concatenate([sides, jnp.zeros((width * 8, depth - quarter), jnp.float32)], axis=1)
    for x in range(width):
        heat[pl.ds(x * (near + 8), near)] = got[x * near : (x + 1) * near]
        heat[pl.ds(x * (near + 8) + near, 8)] = sides[8 * x : 8 * x + 8]


def heating(tile_faces, emission, albedo, cells, about, arrived, width, rows, depth):
    vector = pl.BlockSpec(memory_space=pltpu.VMEM)
    anywhere = pl.BlockSpec(memory_space=pl.ANY)
    return pl.pallas_call(
        functools.partial(heat_kernel, width=width, rows=rows, depth=depth),
        out_shape=(
            jax.ShapeDtypeStruct(emission.shape, jnp.float32),
            jax.ShapeDtypeStruct((width * (rows // 4 + 8), depth), jnp.float32),
        ),
        in_specs=[anywhere] + [vector] * 5,
        out_specs=(vector,) * 2,
        scratch_shapes=[
            pltpu.SMEM(tile_faces.shape, jnp.int32),
            pltpu.SemaphoreType.DMA((1,)),
        ],
        compiler_params=pltpu.CompilerParams(vmem_limit_bytes=32 * 1024 * 1024),
        cost_estimate=pl.CostEstimate(flops=1000, bytes_accessed=1000, transcendentals=0),
        name="heating",
    )(tile_faces, emission, albedo, cells, about, arrived)


def sides_kernel(tile_faces, fields, albedo, cells, first, final, top, bottom, integers, int_sems, sems):
    count, width, rows, depth = fields.shape
    tiles, faces = albedo.shape
    copies = fetched((tile_faces,), (integers,), int_sems)
    for n, (start, buffer) in enumerate(((0, top), (rows - 8, bottom))):
        copy = pltpu.make_async_copy(fields.at[:, :, pl.ds(start, 8)], buffer, sems.at[n])
        copy.start()
        copies.append(copy)
    copies[0].wait()
    for q in range(tiles // HALO):
        live = [live_faces(integers, HALO * q + n, (1, faces)) for n in range(HALO)]
        here = pl.ds(HALO * q, HALO)
        share = 0.1 * jnp.concatenate(live, axis=0) * (1.0 - albedo[here])
        cell = cells[here].astype(jnp.float32)
        for message in (first, final):
            message[count * width + q] = share
            message[count * width + tiles // HALO + q] = cell
    for copy in copies[1:]:
        copy.wait()

    def take(i, carry):
        for n in range(GROUP):
            x = i * GROUP + n
            for f in range(count):
                first[f * width + x] = top[f, x, pl.ds(0, HALO)]
                final[f * width + x] = bottom[f, x, pl.ds(8 - HALO, HALO)]
        return carry

    lax.fori_loop(0, width // GROUP, take, 0)


def sides_of(tile_faces, fields, albedo, cells):
    count, width, rows, depth = fields.shape
    blocks = count * width + 2 * albedo.shape[0] // HALO
    vector = pl.BlockSpec(memory_space=pltpu.VMEM)
    anywhere = pl.BlockSpec(memory_space=pl.ANY)
    message = jax.ShapeDtypeStruct((blocks, HALO, depth), jnp.float32)
    buffer = pltpu.VMEM((count, width, 8, depth), jnp.float32)
    return pl.pallas_call(
        sides_kernel,
        out_shape=(message, message),
        in_specs=[anywhere, anywhere, vector, vector],
        out_specs=(vector, vector),
        scratch_shapes=[
            buffer,
            buffer,
            pltpu.SMEM(tile_faces.shape, jnp.int32),
            pltpu.SemaphoreType.DMA((1,)),
            pltpu.SemaphoreType.DMA((2,)),
        ],
        compiler_params=pltpu.CompilerParams(vmem_limit_bytes=58 * 1024 * 1024),
        cost_estimate=pl.CostEstimate(flops=1000, bytes_accessed=1000, transcendentals=0),
        name="sides",
    )(tile_faces, fields, albedo, cells)


def slabs_kernel(plane_index, fields, after, before, low, high, plane, about, sides, integers, int_sems, sems):
    count, width, rows, depth = fields.shape
    own = pl.ds(0, rows)
    ends = ((low, 0), (high, width - HALO))
    copies = [
        pltpu.make_async_copy(fields.at[:, pl.ds(start, HALO)], slab.at[:, :, own], sems.at[n])
        for n, (slab, start) in enumerate(ends)
    ]
    for n, message in enumerate((after, before)):
        copies.append(pltpu.make_async_copy(message, sides.at[n], sems.at[2 + n]))
    index_copy = fetched((plane_index,), (integers,), int_sems)[0]
    for copy in copies:
        copy.start()
    index_copy.wait()
    p = integers[0, 0]
    copies.append(pltpu.make_async_copy(fields.at[:, p], plane.at[:, own], sems.at[4]))
    copies[-1].start()
    copies[2].wait()
    copies[3].wait()

    def beside(f, x):
        return jnp.concatenate([sides[0, f * width + x], sides[1, f * width + x]], axis=0)

    for n in range(2):
        about[n] = sides[1 - n, pl.ds(count * width, about.shape[1])]
    for f in range(count):
        for slab, start in ends:
            for n in range(HALO):
                slab[f, n, pl.ds(rows, 8)] = beside(f, start + n)
        plane[f, pl.ds(rows, 8)] = beside(f, p)
    for n in (0, 1, 4):
        copies[n].wait()


def slabs_of(plane_index, fields, after, before):
    count, width, rows, depth = fields.shape
    vector = pl.BlockSpec(memory_space=pltpu.VMEM)
    anywhere = pl.BlockSpec(memory_space=pl.ANY)
    slab = jax.ShapeDtypeStruct((count, HALO, rows + 8, depth), jnp.float32)
    return pl.pallas_call(
        slabs_kernel,
        out_shape=(
            slab,
            slab,
            jax.ShapeDtypeStruct((count, rows + 8, depth), jnp.float32),
            jax.ShapeDtypeStruct((2, after.shape[0] - count * width, HALO, depth), jnp.float32),
        ),
        in_specs=[anywhere] * 4,
        out_specs=(vector,) * 4,
        scratch_shapes=[
            pltpu.VMEM((2,) + after.shape, jnp.float32),
            pltpu.SMEM(plane_index.shape, jnp.int32),
            pltpu.SemaphoreType.DMA((1,)),
            pltpu.SemaphoreType.DMA((5,)),
        ],
        compiler_params=pltpu.CompilerParams(vmem_limit_bytes=58 * 1024 * 1024),
        cost_estimate=pl.CostEstimate(flops=1000, bytes_accessed=1000, transcendentals=0),
        name="slabs",
    )(plane_index, fields, after, before)


def local(
    fields,
    emission,
    albedo,
    tile_faces,
    face_cell,
    src_tile,
    dst_tile,
    view_factor,
    pair_count,
    plane_index,
):
    width = fields.shape[1]
    rows = fields.shape[2]
    depth = fields.shape[3]
    n_gx = lax.axis_size("gx")
    n_gy = lax.axis_size("gy")

    integers = tile_faces, src_tile, dst_tile, pair_count
    own = emission[0], albedo[0]
    first, final = sides_of(tile_faces, fields, albedo[0], face_cell[0])
    after = shifted(first, "gy", -1)
    before = shifted(final, "gy", 1)

    outgoing = flux(integers, *own, view_factor[0], n_gy)
    arrived = lax.all_to_all(outgoing, "gy", split_axis=0, concat_axis=0, tiled=True)
    count = fields.shape[0] * width
    yside = jnp.concatenate([after[:count], before[:count]], axis=1).reshape(-1, width, 2 * HALO, depth)
    low, high, plane, about = slabs_of(plane_index[None], fields, after, before)
    plane = shifted(plane, "gx", n_gx // 2, wrap=True).reshape(-1, depth)
    xlow = shifted(high, "gx", 1)
    xhigh = shifted(low, "gx", -1)

    outgoing = flux(integers, *own, view_factor[0], n_gy, arrived)
    outgoing, plane = lax.optimization_barrier((outgoing, plane))
    arrived = lax.all_to_all(outgoing, "gy", split_axis=0, concat_axis=0, tiled=True)
    radiosity, heat = heating(tile_faces, *own, face_cell[0], about, arrived, width, rows, depth)
    relays = shifted(plane, "gx", 1), shifted(plane, "gx", -1)
    heat, *relays = lax.optimization_barrier((heat, *relays))
    near = HALO * (rows // 4 + 8)
    ends = shifted(heat[heat.shape[0] - near :], "gx", 1), shifted(heat[:near], "gx", -1)
    stepped = stencil(fields, yside, xlow, xhigh, plane, *relays, heat, *ends)
    return (stepped, radiosity[None])


def solution(mesh):
    return jax.shard_map(
        local,
        mesh=mesh,
        in_specs=(
            P(None, "gx", "gy", None),
            P("gx", "gy", None, None),
            P("gx", "gy", None),
            P("gx", "gy"),
            P("gx", "gy", None),
            P("gx", "gy"),
            P("gx", "gy"),
            P("gx", "gy", None, None),
            P("gx", "gy"),
            P("gx"),
        ),
        out_specs=(P(None, "gx", "gy", None), P("gx", "gy", None, None)),
        check_vma=False,
    )
```

```python
import functools

import jax
import jax.numpy as jnp
from jax import lax
from jax.experimental import pallas as pl
from jax.experimental.pallas import tpu as pltpu
from jax.sharding import PartitionSpec as P

STEPS = 4
HALO = STEPS
CHUNK = 8
GROUP = 4


def shifted(value, axis, steps, wrap=False):
    count = lax.axis_size(axis)
    pairs = [(i, (i + steps) % count) for i in range(count) if wrap or 0 <= i + steps < count]
    return lax.ppermute(value, axis, pairs)


def stencil_kernel(
    fields, yside, xlow, xhigh, plane, relay_low, relay_high, heat, end_low, end_high, out,
    a, b, rec, packed, src, in_sems, out_sems, *, width, rows
):
    fields_n = fields.shape[0]
    tiles = rows // 8 + 1
    chunks = width // CHUNK
    total = width + 2 * HALO
    gx = lax.axis_index("gx")
    gy = lax.axis_index("gy")
    last_gx = lax.axis_size("gx") - 1
    last_gy = lax.axis_size("gy") - 1

    def own_copy(k):
        return pltpu.make_async_copy(
            fields.at[:, pl.ds(k * CHUNK, CHUNK)],
            a.at[:, pl.ds(HALO + k * CHUNK, CHUNK), pl.ds(0, rows)],
            in_sems.at[0, k],
        )

    def side_copy(k):
        return pltpu.make_async_copy(
            yside.at[:, pl.ds(k * CHUNK, CHUNK)],
            a.at[:, pl.ds(HALO + k * CHUNK, CHUNK), pl.ds(rows, 8)],
            in_sems.at[1, k],
        )

    def out_copy(k):
        return pltpu.make_async_copy(
            a.at[:, pl.ds(HALO + k * CHUNK, CHUNK), pl.ds(0, rows)],
            out.at[:, pl.ds(k * CHUNK, CHUNK)],
            out_sems.at[k],
        )

    low_copy = pltpu.make_async_copy(
        xlow, a.at[:, pl.ds(0, HALO)], in_sems.at[2, 0]
    )
    high_copy = pltpu.make_async_copy(
        xhigh, a.at[:, pl.ds(HALO + width, HALO)], in_sems.at[2, 1]
    )
    heat_rows = rows // 4 + 8
    near = HALO * heat_rows
    plane_copies = [
        pltpu.make_async_copy(relay_low, rec.at[0], in_sems.at[2, 2]),
        pltpu.make_async_copy(plane, rec.at[1], in_sems.at[2, 3]),
        pltpu.make_async_copy(relay_high, rec.at[2], in_sems.at[2, 4]),
    ]
    heat_copies = [
        pltpu.make_async_copy(heat, packed.at[pl.ds(near, width * heat_rows)], in_sems.at[3, 0]),
        pltpu.make_async_copy(end_low, packed.at[pl.ds(0, near)], in_sems.at[3, 1]),
        pltpu.make_async_copy(
            end_high, packed.at[pl.ds(near + width * heat_rows, near)], in_sems.at[3, 2]
        ),
    ]
    for copy in heat_copies + plane_copies:
        copy.start()
    low_copy.start()
    for k in range(chunks):
        own_copy(k).start()
        side_copy(k).start()
    high_copy.start()

    zero = jnp.zeros((8, a.shape[-1]), jnp.float32)
    for f in range(fields_n):
        for j in range(tiles):
            b[f, HALO - 1, pl.ds(8 * j, 8)] = zero
            b[f, HALO + width, pl.ds(8 * j, 8)] = zero
    row = lax.broadcasted_iota(jnp.int32, zero.shape, 0)
    lane = lax.broadcasted_iota(jnp.int32, zero.shape, 1)
    depth = zero.shape[1]
    for copy in heat_copies:
        copy.wait()

    def unpack(i, carry):
        quarter = depth // 4
        for n in range(CHUNK):
            x = i * CHUNK + n
            for half in range(rows // 32):
                block = packed[pl.ds(x * heat_rows + 8 * half, 8)]
                for q in range(4):
                    part = pltpu.roll(block, depth - q * quarter, 1) if q else block
                    src[x, pl.ds(q * (rows // 4) + 8 * half, 8)] = jnp.where(lane < quarter, part, 0.0)
            src[x, pl.ds(rows, 8)] = packed[pl.ds(x * heat_rows + rows // 4, 8)]
        return carry

    lax.fori_loop(0, total // CHUNK, unpack, 0)
    for copy in plane_copies:
        copy.wait()
    for s in range(3):
        for r in range(fields_n * tiles):
            rec[s, pl.ds(8 * r, 8)] = 0.05 * rec[s, pl.ds(8 * r, 8)]
    low_copy.wait()

    first_row = row == 0
    final_row = row == 7
    up = jnp.where(lane == depth - 1, 0.0, 1.0).astype(jnp.float32)
    down = jnp.where(lane == 0, 0.0, 1.0).astype(jnp.float32)
    after = (row < 4) & (gy < last_gy)
    before = (row >= 4) & (gy > 0)
    side_mask = jnp.where(after | before, 1.0, 0.0).astype(jnp.float32)

    def planes_step(old, new, x, slots, last):
        count = tiles - 1 if last else tiles
        for j in range(count):
            here = pl.ds(8 * j, 8)
            above = pl.ds(8 * ((j + 1) % tiles), 8)
            below = pl.ds(8 * ((j - 1) % tiles), 8)
            columns = [[old[f, x + n, here] for n in range(-1, GROUP + 1)] for f in range(fields_n)]
            for n in range(GROUP):
                at = n + 1
                u = 0.05 * columns[2][at]
                v = 0.05 * columns[3][at]
                w = 0.05 * columns[4][at]
                c_xp, c_xm = 0.02 - u, 0.02 + u
                c_yp, c_ym = 0.02 - v, 0.02 + v
                c_zp, c_zm = up * (0.02 - w), down * (0.02 + w)
                for f in range(fields_n):
                    c = columns[f][at]
                    if j < tiles - 1:
                        yp = old[f, x + n, pl.ds(8 * j + 1, 8)]
                    else:
                        yp = jnp.where(final_row, pltpu.roll(old[f, x + n, above], 7, 0), pltpu.roll(c, 7, 0))
                    if j > 0:
                        ym = old[f, x + n, pl.ds(8 * j - 1, 8)]
                    else:
                        ym = jnp.where(first_row, pltpu.roll(old[f, x + n, below], 1, 0), pltpu.roll(c, 1, 0))
                    t1 = 0.83 * c + rec[slots[n], pl.ds(8 * (f * tiles + j), 8)]
                    t2 = c_xp * columns[f][at + 1] + c_xm * columns[f][at - 1]
                    t3 = c_yp * yp + c_ym * ym
                    t4 = c_zp * pltpu.roll(c, depth - 1, 1) + c_zm * pltpu.roll(c, 1, 1)
                    value = (t1 + t2) + (t3 + t4)
                    if f == 0:
                        value = value + src[x + n, here]
                    if j == tiles - 1:
                        value = value * side_mask
                    new[f, x + n, here] = value

    own_copy(0).wait()
    side_copy(0).wait()
    for step in range(1, STEPS + 1):
        old, new = (a, b) if step % 2 == 1 else (b, a)
        first = jnp.where(gx == 0, HALO, step)
        end = jnp.where(gx == last_gx, HALO + width, total - step)

        def body(i, carry, old=old, new=new, step=step, first=first, end=end):
            x = jnp.minimum(first + GROUP * i, end - GROUP)
            if step == 1:
                part = lax.div(x + GROUP - HALO + CHUNK, CHUNK) - 1
                past = lax.div(first + GROUP * i - HALO + CHUNK, CHUNK) - 1

                @pl.when((part > past) & (part > 0) & (part < chunks))
                def _():
                    own_copy(part).wait()
                    side_copy(part).wait()

                @pl.when((part > past) & (part == chunks))
                def _():
                    high_copy.wait()

            def slot(n):
                if step == STEPS:
                    return 1
                return jnp.where(x + n < HALO, 0, jnp.where(x + n < HALO + width, 1, 2))

            planes_step(old, new, x, [slot(n) for n in range(GROUP)], step == STEPS)
            if step == STEPS:
                done = x + GROUP - HALO

                @pl.when(lax.rem(done, CHUNK) == 0)
                def _():
                    out_copy(lax.div(done, CHUNK) - 1).start()

            return carry

        lax.fori_loop(0, lax.div(end - first + GROUP - 1, GROUP), body, 0)
    for k in range(chunks):
        out_copy(k).wait()


def stencil(fields, *others):
    count, width, rows, depth = fields.shape
    total = width + 2 * HALO
    buffer = pltpu.VMEM((count, total, rows + 8, depth), jnp.float32)
    return pl.pallas_call(
        functools.partial(stencil_kernel, width=width, rows=rows),
        out_shape=jax.ShapeDtypeStruct(fields.shape, jnp.float32),
        in_specs=[pl.BlockSpec(memory_space=pl.ANY)] * 10,
        out_specs=pl.BlockSpec(memory_space=pl.ANY),
        scratch_shapes=[
            buffer,
            buffer,
            pltpu.VMEM((3, count * (rows + 8), depth), jnp.float32),
            pltpu.VMEM((total * (rows // 4 + 8), depth), jnp.float32),
            pltpu.VMEM((total, rows + 8, depth), jnp.float32),
            pltpu.SemaphoreType.DMA((4, max(width // CHUNK, 5))),
            pltpu.SemaphoreType.DMA((width // CHUNK,)),
        ],
        compiler_params=pltpu.CompilerParams(vmem_limit_bytes=48 * 1024 * 1024),
        cost_estimate=pl.CostEstimate(flops=160_000_000, bytes_accessed=20_000_000, transcendentals=0),
        name="stencil",
    )(fields, *others)


NT = (((1,), (1,)), ((), ()))
PAIR_CHUNK = 8


def split(value):
    high = value.astype(jnp.bfloat16)
    return high, (value - high.astype(jnp.float32)).astype(jnp.bfloat16)


def live_faces(counts, t, shape):
    lane = lax.broadcasted_iota(jnp.int32, shape, 1)
    return jnp.where(lane < counts[0, t], 1.0, 0.0).astype(jnp.float32)


def summed(arrived, block, blocks):
    total = arrived[block]
    for g in range(1, arrived.shape[0] // blocks):
        total = total + arrived[g * blocks + block]
    return total


def fetched(arrays, scratch, sems):
    copies = [pltpu.make_async_copy(a, s, sems.at[n]) for n, (a, s) in enumerate(zip(arrays, scratch))]
    for copy in copies:
        copy.start()
    return copies


def flux_kernel(tile_faces, sources, targets, count, emission, albedo, factors, *rest, devices, last, beside=None):
    arrived, (out, held, lhs, *integers, int_sems, sems) = (rest[0] if last else None), rest[last:]
    tiles, bands, faces = emission.shape
    pairs = factors.shape[0]
    chunks = pairs // PAIR_CHUNK
    blocks = out.shape[0] // devices

    def chunk_copy(k):
        part = pl.ds(k * PAIR_CHUNK, PAIR_CHUNK)
        return pltpu.make_async_copy(factors.at[part], held.at[part], sems.at[k])

    copies = fetched((tile_faces, sources, targets, count), integers, int_sems)
    for k in range(chunks):
        chunk_copy(k).start()
    out[...] = jnp.zeros_like(out)
    for copy in copies:
        copy.wait()
    tile_faces, sources, targets, count = integers
    for t in range(tiles):
        radiosity = emission[t]
        if last:
            radiosity = radiosity + albedo[pl.ds(t, 1), :] * summed(arrived, t, tiles)
        radiosity = live_faces(tile_faces, t, (bands, faces)) * radiosity
        high, low = split(radiosity)
        high, low = high.astype(jnp.float32), low.astype(jnp.float32)
        nothing = jnp.zeros_like(high)
        left = jnp.concatenate([high, low, nothing, nothing], axis=0)
        right = jnp.concatenate([high, nothing, nothing, nothing], axis=0)
        lhs[t] = jnp.concatenate([left, right], axis=1).astype(jnp.bfloat16)

    if beside is not None:
        beside(tile_faces)

    def chunk_step(k, carry):
        chunk_copy(k).wait()
        for i in range(PAIR_CHUNK // 2):
            first = k * PAIR_CHUNK + 2 * i
            both = held[pl.ds(first, 2)].reshape(2 * faces, faces)
            rhs = jnp.concatenate(split(both), axis=1)
            rows = [lhs[sources[0, first + n]] for n in range(2)]
            got = lax.dot_general(jnp.concatenate(rows, axis=0), rhs, NT, preferred_element_type=jnp.float32)
            for n in range(2):
                part = got[16 * n : 16 * n + 8, n * faces : (n + 1) * faces]
                flux = part[:bands] + part[bands : 2 * bands]
                target = targets[0, first + n]
                if last:
                    target = lax.div(target, tiles) * blocks + lax.rem(target, tiles)
                out[target] = out[target] + jnp.where(first + n < count[0, 0], flux, 0.0)
        return carry

    lax.fori_loop(0, chunks, chunk_step, 0)
    if last:
        groups = tiles // bands
        for e in range(devices):
            for q in range(groups):
                sums = [
                    jnp.sum(out[e * blocks + q * bands + n], axis=0, keepdims=True) for n in range(bands)
                ]
                sums = jnp.concatenate(sums, axis=0)
                if e + 1 < devices:
                    out[(e + 1) * blocks + tiles + q] = sums
                if e > 0:
                    out[(e - 1) * blocks + tiles + groups + q] = sums


def flux(integers, emission, albedo, factors, devices, arrived=None):
    tiles, bands, faces = emission.shape
    pairs = factors.shape[0]
    last = arrived is not None
    blocks = tiles + (2 * tiles // bands if last else 0)
    vector = pl.BlockSpec(memory_space=pltpu.VMEM)
    anywhere = pl.BlockSpec(memory_space=pl.ANY)
    return pl.pallas_call(
        functools.partial(flux_kernel, devices=devices, last=last),
        out_shape=jax.ShapeDtypeStruct((devices * blocks, bands, faces), jnp.float32),
        in_specs=[anywhere] * 4 + [vector, vector, anywhere] + [vector] * last,
        out_specs=vector,
        scratch_shapes=[
            pltpu.VMEM(factors.shape, jnp.float32),
            pltpu.VMEM((tiles, 16, 2 * faces), jnp.bfloat16),
            *[pltpu.SMEM(a.shape, jnp.int32) for a in integers],
            pltpu.SemaphoreType.DMA((len(integers),)),
            pltpu.SemaphoreType.DMA((pairs // PAIR_CHUNK,)),
        ],
        compiler_params=pltpu.CompilerParams(vmem_limit_bytes=60 * 1024 * 1024),
        cost_estimate=pl.CostEstimate(flops=1000, bytes_accessed=1000, transcendentals=0),
        name="flux",
    )(*integers, emission, albedo, factors, *([arrived] if last else []))


def one_hot(count, index):
    at = lax.broadcasted_iota(jnp.int32, (count, index.shape[1]), 0) == index
    return at


def weighed(count, index, value):
    at = one_hot(count, index)
    top = value.astype(jnp.bfloat16).astype(jnp.float32)
    both = [jnp.where(at, top, 0.0), jnp.where(at, value - top, 0.0)]
    return jnp.concatenate(both, axis=0).astype(jnp.bfloat16)


def picked(count, index):
    return jnp.where(one_hot(count, index), 1.0, 0.0).astype(jnp.bfloat16)


def heat_kernel(
    tile_faces, emission, albedo, cells, about, arrived, radiosity, heat, integers, int_sems, *, width, rows, depth
):
    tiles, bands, faces = emission.shape
    quarter = depth // 4
    near = rows // 4
    blocks = tiles + 2 * tiles // bands
    level_bits = depth.bit_length() - 1
    row_bits = rows.bit_length() - 1

    fetched((tile_faces,), (integers,), int_sems)[0].wait()
    tile_faces = integers

    def place(cell):
        return cell >> (level_bits + row_bits), (cell >> level_bits) & (rows - 1), cell & (depth - 1)

    picks, weights = [], []
    for t in range(tiles):
        live = live_faces(tile_faces, t, (bands, faces))
        incoming = summed(arrived, t, blocks)
        share = albedo[pl.ds(t, 1), :]
        radiosity[t] = live * (emission[t] + share * incoming)
        absorbed = 0.1 * live[:1] * (1.0 - share) * jnp.sum(incoming, axis=0, keepdims=True)
        x, y, level = place(cells[pl.ds(t, 1), :])
        picks.append(picked(width * near, x * near + (y & (near - 1))))
        weights.append(weighed(depth, (y // near) * quarter + level, absorbed))
    got = lax.dot_general(
        jnp.concatenate(picks, axis=1), jnp.concatenate(weights, axis=1), NT, preferred_element_type=jnp.float32
    )
    got = got[:, :depth] + got[:, depth:]

    picks, weights = [], []
    groups = tiles // bands
    for side in range(2):
        for q in range(groups):
            incoming = summed(arrived, tiles + side * groups + q, blocks)
            absorbed = about[side, q] * incoming
            cell = about[side, groups + q].astype(jnp.int32)
            for n in range(bands):
                x, y, level = place(cell[n : n + 1])
                if side:
                    row = jnp.where(y < HALO, x * 8 + y, -1)
                else:
                    row = jnp.where(y >= rows - HALO, x * 8 + HALO + y - (rows - HALO), -1)
                picks.append(picked(width * 8, row))
                weights.append(weighed(quarter, level, absorbed[n : n + 1]))
    sides = lax.dot_general(
        jnp.concatenate(picks, axis=1), jnp.concatenate(weights, axis=1), NT, preferred_element_type=jnp.float32
    )
    sides = sides[:, :quarter] + sides[:, quarter:]
    sides = jnp.concatenate([sides, jnp.zeros((width * 8, depth - quarter), jnp.float32)], axis=1)
    for x in range(width):
        heat[pl.ds(x * (near + 8), near)] = got[x * near : (x + 1) * near]
        heat[pl.ds(x * (near + 8) + near, 8)] = sides[8 * x : 8 * x + 8]


def heating(tile_faces, emission, albedo, cells, about, arrived, width, rows, depth):
    vector = pl.BlockSpec(memory_space=pltpu.VMEM)
    anywhere = pl.BlockSpec(memory_space=pl.ANY)
    return pl.pallas_call(
        functools.partial(heat_kernel, width=width, rows=rows, depth=depth),
        out_shape=(
            jax.ShapeDtypeStruct(emission.shape, jnp.float32),
            jax.ShapeDtypeStruct((width * (rows // 4 + 8), depth), jnp.float32),
        ),
        in_specs=[anywhere] + [vector] * 5,
        out_specs=(vector,) * 2,
        scratch_shapes=[
            pltpu.SMEM(tile_faces.shape, jnp.int32),
            pltpu.SemaphoreType.DMA((1,)),
        ],
        compiler_params=pltpu.CompilerParams(vmem_limit_bytes=32 * 1024 * 1024),
        cost_estimate=pl.CostEstimate(flops=1000, bytes_accessed=1000, transcendentals=0),
        name="heating",
    )(tile_faces, emission, albedo, cells, about, arrived)


def opening_kernel(
    tile_faces, sources, targets, count, emission, albedo, factors, fields, cells, out, first, final,
    held, lhs, tile_faces_, sources_, targets_, count_, int_sems, sems, edges, messages, edge_sems, *, devices
):
    fields_n, width, rows, depth = fields.shape
    tiles, faces = albedo.shape
    inward = [
        pltpu.make_async_copy(fields.at[:, :, pl.ds(start, 8)], edges.at[n], edge_sems.at[n])
        for n, start in enumerate((0, rows - 8))
    ]
    outward = [
        pltpu.make_async_copy(messages.at[n], message, edge_sems.at[2 + n]) for n, message in enumerate((first, final))
    ]
    for copy in inward:
        copy.start()

    def pack(live_counts):
        for q in range(tiles // HALO):
            live = [live_faces(live_counts, HALO * q + n, (1, faces)) for n in range(HALO)]
            here = pl.ds(HALO * q, HALO)
            share = 0.1 * jnp.concatenate(live, axis=0) * (1.0 - albedo[here])
            cell = cells[here].astype(jnp.float32)
            for n in range(2):
                messages[n, fields_n * width + q] = share
                messages[n, fields_n * width + tiles // HALO + q] = cell

        for side, start in enumerate((0, 8 - HALO)):
            inward[side].wait()

            def take(i, carry, side=side, start=start):
                for n in range(GROUP):
                    x = i * GROUP + n
                    for f in range(fields_n):
                        messages[side, f * width + x] = edges[side, f, x, pl.ds(start, HALO)]
                return carry

            lax.fori_loop(0, width // GROUP, take, 0)
            outward[side].start()

    flux_kernel(
        tile_faces, sources, targets, count, emission, albedo, factors, out, held, lhs,
        tile_faces_, sources_, targets_, count_, int_sems, sems, devices=devices, last=False, beside=pack,
    )
    for copy in outward:
        copy.wait()


def opening(integers, emission, albedo, factors, fields, cells, devices):
    tiles, bands, faces = emission.shape
    pairs = factors.shape[0]
    count, width, rows, depth = fields.shape
    blocks = count * width + 2 * tiles // HALO
    vector = pl.BlockSpec(memory_space=pltpu.VMEM)
    anywhere = pl.BlockSpec(memory_space=pl.ANY)
    message = jax.ShapeDtypeStruct((blocks, HALO, depth), jnp.float32)
    return pl.pallas_call(
        functools.partial(opening_kernel, devices=devices),
        out_shape=(jax.ShapeDtypeStruct((devices * tiles, bands, faces), jnp.float32), message, message),
        in_specs=[anywhere] * 4 + [vector, vector, anywhere, anywhere, vector],
        out_specs=(vector, anywhere, anywhere),
        scratch_shapes=[
            pltpu.VMEM(factors.shape, jnp.float32),
            pltpu.VMEM((tiles, 16, 2 * faces), jnp.bfloat16),
            *[pltpu.SMEM(a.shape, jnp.int32) for a in integers],
            pltpu.SemaphoreType.DMA((len(integers),)),
            pltpu.SemaphoreType.DMA((pairs // PAIR_CHUNK,)),
            pltpu.VMEM((2, count, width, 8, depth), jnp.float32),
            pltpu.VMEM((2,) + message.shape, jnp.float32),
            pltpu.SemaphoreType.DMA((4,)),
        ],
        compiler_params=pltpu.CompilerParams(vmem_limit_bytes=60 * 1024 * 1024),
        cost_estimate=pl.CostEstimate(flops=1000, bytes_accessed=1000, transcendentals=0),
        name="opening",
    )(*integers, emission, albedo, factors, fields, cells)


def slabs_kernel(plane_index, fields, after, before, low, high, plane, about, sides, integers, int_sems, sems):
    count, width, rows, depth = fields.shape
    own = pl.ds(0, rows)
    ends = ((low, 0), (high, width - HALO))
    copies = [
        pltpu.make_async_copy(fields.at[:, pl.ds(start, HALO)], slab.at[:, :, own], sems.at[n])
        for n, (slab, start) in enumerate(ends)
    ]
    for n, message in enumerate((after, before)):
        copies.append(pltpu.make_async_copy(message, sides.at[n], sems.at[2 + n]))
    index_copy = fetched((plane_index,), (integers,), int_sems)[0]
    for copy in copies:
        copy.start()
    index_copy.wait()
    p = integers[0, 0]
    copies.append(pltpu.make_async_copy(fields.at[:, p], plane.at[:, own], sems.at[4]))
    copies[-1].start()
    copies[2].wait()
    copies[3].wait()

    def beside(f, x):
        return jnp.concatenate([sides[0, f * width + x], sides[1, f * width + x]], axis=0)

    for n in range(2):
        about[n] = sides[1 - n, pl.ds(count * width, about.shape[1])]
    for f in range(count):
        for slab, start in ends:
            for n in range(HALO):
                slab[f, n, pl.ds(rows, 8)] = beside(f, start + n)
        plane[f, pl.ds(rows, 8)] = beside(f, p)
    for n in (0, 1, 4):
        copies[n].wait()


def slabs_of(plane_index, fields, after, before):
    count, width, rows, depth = fields.shape
    vector = pl.BlockSpec(memory_space=pltpu.VMEM)
    anywhere = pl.BlockSpec(memory_space=pl.ANY)
    slab = jax.ShapeDtypeStruct((count, HALO, rows + 8, depth), jnp.float32)
    return pl.pallas_call(
        slabs_kernel,
        out_shape=(
            slab,
            slab,
            jax.ShapeDtypeStruct((count, rows + 8, depth), jnp.float32),
            jax.ShapeDtypeStruct((2, after.shape[0] - count * width, HALO, depth), jnp.float32),
        ),
        in_specs=[anywhere] * 4,
        out_specs=(vector,) * 4,
        scratch_shapes=[
            pltpu.VMEM((2,) + after.shape, jnp.float32),
            pltpu.SMEM(plane_index.shape, jnp.int32),
            pltpu.SemaphoreType.DMA((1,)),
            pltpu.SemaphoreType.DMA((5,)),
        ],
        compiler_params=pltpu.CompilerParams(vmem_limit_bytes=58 * 1024 * 1024),
        cost_estimate=pl.CostEstimate(flops=1000, bytes_accessed=1000, transcendentals=0),
        name="slabs",
    )(plane_index, fields, after, before)


def local(
    fields,
    emission,
    albedo,
    tile_faces,
    face_cell,
    src_tile,
    dst_tile,
    view_factor,
    pair_count,
    plane_index,
):
    width = fields.shape[1]
    rows = fields.shape[2]
    depth = fields.shape[3]
    n_gx = lax.axis_size("gx")
    n_gy = lax.axis_size("gy")

    integers = tile_faces, src_tile, dst_tile, pair_count
    own = emission[0], albedo[0]
    outgoing, first, final = opening(integers, *own, view_factor[0], fields, face_cell[0], n_gy)
    after = shifted(first, "gy", -1)
    before = shifted(final, "gy", 1)

    arrived = lax.all_to_all(outgoing, "gy", split_axis=0, concat_axis=0, tiled=True)
    count = fields.shape[0] * width
    yside = jnp.concatenate([after[:count], before[:count]], axis=1).reshape(-1, width, 2 * HALO, depth)
    low, high, plane, about = slabs_of(plane_index[None], fields, after, before)
    plane = shifted(plane, "gx", n_gx // 2, wrap=True).reshape(-1, depth)
    xlow = shifted(high, "gx", 1)
    xhigh = shifted(low, "gx", -1)

    outgoing = flux(integers, *own, view_factor[0], n_gy, arrived)
    arrived = lax.all_to_all(outgoing, "gy", split_axis=0, concat_axis=0, tiled=True)
    radiosity, heat = heating(tile_faces, *own, face_cell[0], about, arrived, width, rows, depth)
    relays = shifted(plane, "gx", 1), shifted(plane, "gx", -1)
    heat, *relays = lax.optimization_barrier((heat, *relays))
    near = HALO * (rows // 4 + 8)
    ends = shifted(heat[heat.shape[0] - near :], "gx", 1), shifted(heat[:near], "gx", -1)
    stepped = stencil(fields, yside, xlow, xhigh, plane, *relays, heat, *ends)
    return (stepped, radiosity[None])


def solution(mesh):
    return jax.shard_map(
        local,
        mesh=mesh,
        in_specs=(
            P(None, "gx", "gy", None),
            P("gx", "gy", None, None),
            P("gx", "gy", None),
            P("gx", "gy"),
            P("gx", "gy", None),
            P("gx", "gy"),
            P("gx", "gy"),
            P("gx", "gy", None, None),
            P("gx", "gy"),
            P("gx"),
        ),
        out_specs=(P(None, "gx", "gy", None), P("gx", "gy", None, None)),
        check_vma=False,
    )
```
